512 devices in a mesh: section: 16 (over x, y), ctx: 32 (over z, core).
Axes of the slice: x: 4, y: 4, z: 16, core: 2. Of those that a mesh axis runs over, the one named last changes fastest.
Arguments:
- activations: bfloat16 [16, 4096, 1024], P('section', 'ctx'), may hold values from -6 to 6
- norm_gain: float32 [16, 1024], P('section'), may hold values from 0.5 to 1.5
- in_weight: bfloat16 [16, 1024, 3072], P('section', 'ctx'), may hold values from -0.1875 to 0.1875
- short_weight: float32 [16, 3, 3072], P('section'), may hold values from -1 to 1
- long_filter: float32 [16, 1024, 4096], P('section', 'ctx'), may hold values from -1.2 to 1.2, as said below
- out_weight: bfloat16 [16, 1024, 1024], P('section', None, 'ctx'), may hold values from -0.1875 to 0.1875
Outputs:
- block_out: bfloat16 [16, 4096, 1024], P('section', 'ctx')
The draws below stay inside these ranges and needn't reach their ends.
Inputs may be any that keep to these rules, and one draw needn't show every extreme that they name: `long_filter`: a causal filter whose magnitude falls with the lag at a rate that varies over channels.
All inputs are finite; a program needn't handle non-finite values.
Results may differ from the reference program's by a relative error of at most 0.0051.
Values may be sent and summed in bfloat16 or wider, within the bound.
A program may use at most 64 MiB of HBM per device.

```python
import math
import jax
import jax.numpy as jnp
from jax import lax

FEATURE_WIDTH = 1024
KERNEL = 3
SEQUENCE_SIZE = 4096
DEVICE_PARTS = 16


def draw_long_filter(key, part):
    key = jax.random.fold_in(key, 11)
    random_seeds = jax.random.split(key, 4)
    kernel_delays = jnp.arange(SEQUENCE_SIZE, dtype=jnp.float32)[None, None, :]
    clutter_extents = jnp.exp(jax.random.uniform(random_seeds[0], (DEVICE_PARTS, FEATURE_WIDTH, 1), jnp.float32, math.log(30.0), math.log(64.0 * SEQUENCE_SIZE)))
    waveform_height = 1.0 / jnp.sqrt(jnp.minimum(clutter_extents / 2.0 + 1.0, SEQUENCE_SIZE * 1.0))
    jagged_waveform = jax.random.truncated_normal(random_seeds[1], -4.0, 4.0, (DEVICE_PARTS, FEATURE_WIDTH, SEQUENCE_SIZE), jnp.float32)
    dropout_places = jax.random.randint(random_seeds[2], (DEVICE_PARTS, 1, 1, 3), 0, SEQUENCE_SIZE)
    waveform_gaps = jax.random.uniform(random_seeds[3], (DEVICE_PARTS, FEATURE_WIDTH, 1, 3), jnp.float32, 0.5, 0.8)
    random_clutter = jnp.ones((DEVICE_PARTS, FEATURE_WIDTH, SEQUENCE_SIZE), jnp.float32)
    sequence_offsets = jnp.arange(SEQUENCE_SIZE, dtype=jnp.int32)[None, None, :]
    for chosen_slot in range(3):
        random_clutter = random_clutter * jnp.where(sequence_offsets >= dropout_places[..., chosen_slot], waveform_gaps[..., chosen_slot], 1.0)
    return waveform_height * jnp.exp(-kernel_delays / clutter_extents) * random_clutter * jagged_waveform


def block_levels(key, shape, pieces, low, top_value):
    level, own = 1.0, jax.random.fold_in(key, 6)
    for dim, blocks in pieces:
        heights = jnp.exp(jax.random.uniform(jax.random.fold_in(own, dim), (blocks,), jnp.float32, low / len(pieces), top_value / len(pieces)))
        level = level * jnp.repeat(heights, shape[dim] // blocks).reshape([-1 if axis == dim else 1 for axis in range(len(shape))])
    return level


def centred(stream_key, shape, scale, most, cuts=(), kind=jnp.bfloat16):
    factor_of = block_levels(stream_key, shape, cuts, -0.22, 0.18) if cuts else 1.0
    entries = jax.random.normal(stream_key, shape, jnp.float32) * scale * factor_of
    return jnp.minimum(jnp.maximum(entries, -most), most).astype(kind)


def setup_inputs(seed: int = 0) -> dict:
    key_of = jax.random.split(jax.random.key(seed), 7)
    return {
        "activations": centred(key_of[0], (DEVICE_PARTS, SEQUENCE_SIZE, FEATURE_WIDTH), 1.0, 6.0, ((0, 16), (1, 32))),
        "norm_gain": jnp.clip(1.0 + 0.1 * jax.random.normal(key_of[1], (DEVICE_PARTS, FEATURE_WIDTH), jnp.float32), 0.5, 1.5),
        "in_weight": centred(key_of[2], (DEVICE_PARTS, FEATURE_WIDTH, 3 * FEATURE_WIDTH), FEATURE_WIDTH ** -0.5, 0.1875, ((0, 16), (1, 32))),
        "short_weight": jnp.clip(jax.random.uniform(key_of[3], (DEVICE_PARTS, KERNEL, 3 * FEATURE_WIDTH), jnp.float32, -1.0, 1.0) * block_levels(key_of[3], (DEVICE_PARTS, KERNEL, 3 * FEATURE_WIDTH), ((0, 16),), -0.4, 0.0), -1.0, 1.0),
        "long_filter": draw_long_filter(jax.random.fold_in(key_of[6], 71), 0),
        "out_weight": centred(key_of[5], (DEVICE_PARTS, FEATURE_WIDTH, FEATURE_WIDTH), FEATURE_WIDTH ** -0.5, 0.1875, ((0, 16), (2, 32))),
    }


highest = lax.Precision.HIGHEST

def one_section(section_in, gain_row, in_proj, short_taps, filter_rows, out_proj):
    values = section_in.astype(jnp.float32)
    scale = lax.rsqrt(lax.optimization_barrier(jnp.mean(values * values, axis=-1, keepdims=True)) + 1e-06)
    normed = (values * scale * gain_row).astype(jnp.bfloat16)
    features = jnp.dot(normed.astype(jnp.float32), in_proj.astype(jnp.float32), precision=highest)
    padded = jnp.pad(features, ((2, 0), (0, 0)))
    mixed = short_taps[0] * features + short_taps[1] * padded[1:-1] + short_taps[2] * padded[:-2]
    model_width = section_in.shape[1]
    query_side = mixed[:, :model_width]
    key_side = mixed[:, model_width:2 * model_width]
    value_side = mixed[:, 2 * model_width:]
    product = (key_side * value_side).astype(jnp.bfloat16).astype(jnp.float32)
    length = section_in.shape[0]
    spec_data = jnp.fft.rfft(product, n=2 * length, axis=0)
    spec_filter = jnp.fft.rfft(jnp.transpose(filter_rows), n=2 * length, axis=0)
    conv = jnp.fft.irfft(spec_data * spec_filter, n=2 * length, axis=0)[:length]
    conv = conv.astype(jnp.float32).astype(jnp.bfloat16)
    gated = (query_side * conv.astype(jnp.float32)).astype(jnp.bfloat16)
    mixing = jnp.dot(gated.astype(jnp.float32), out_proj.astype(jnp.float32), precision=highest)
    return (values + mixing).astype(jnp.bfloat16)

def reference(activations, norm_gain, in_weight, short_weight, long_filter, out_weight):
    inputs = jnp.roll(activations, 1, axis=0)

    def apply(packed):
        return one_section(*packed)
    return lax.map(apply, (inputs, norm_gain, in_weight, short_weight, long_filter, out_weight))
```

```python
import functools
import math

import jax
import jax.numpy as jnp
import numpy as np
from jax import lax
from jax.experimental import pallas as pl
from jax.experimental.pallas import tpu as pltpu
from jax.sharding import PartitionSpec as P

MESH = pl.DeviceIdType.MESH
F32, BF16 = jnp.float32, jnp.bfloat16
HALO = 16
HALF = 16


def transform_tables(parts, block):
    points = parts * block
    k = np.arange(parts)[:, None] + 0.25
    outer = 2.0 * math.pi * k * np.arange(parts)[None, :] / parts
    eye = np.eye(HALF)
    forward = np.concatenate([np.kron(np.cos(outer), eye), np.kron(-np.sin(outer), eye)], axis=0)
    inner = 2.0 * math.pi * np.outer(np.arange(block), np.arange(block)) / block
    cos, sin = np.cos(inner), np.sin(inner)
    inner_forward = np.block([[cos, -sin], [sin, cos]])
    inner_inverse = np.block([[cos, sin], [-sin, cos]])
    twist = np.repeat(2.0 * math.pi * k * np.arange(block)[None, :] / points, HALF, axis=0)
    tables = (forward, forward.T, inner_forward, inner_inverse, np.cos(twist), np.sin(twist))
    return [np.asarray(table, np.float32) for table in tables]


def split(value):
    high = value.astype(BF16)
    return high, (value - high.astype(F32)).astype(BF16)


def dot(a, b):
    return jnp.dot(a, b, preferred_element_type=F32)


def dot3(a_high, a_low, b_high, b_low):
    return dot(a_high, b_high) + (dot(a_high, b_low) + dot(a_low, b_high))


def kernel(
    sections, chips, width, tokens,
    act, gain, in_w, taps, filt, out_w, g_in, gi_in, d_in, di_in, tw_cos_in, tw_sin_in,
    out,
    w, rows_in, halo_in, normed, feat, prod, chan, query, outer, spec, back_hi, back_lo, conv, ret,
    fil, g_all, gi_all, d_all, di_all, tw_cos, tw_sin, g_hi, g_lo, gi_hi, gi_lo, d_hi, d_lo, di_hi, di_lo,
    ring_send, ring_recv, own_sem, relay_send, relay_recv, to_send, to_recv, back_send, back_recv,
    load_sem,
):
    parts = 2 * chips
    depth = width // parts
    block = tokens
    half_rows = parts * HALF
    tile = min(256, width)
    sec, me = lax.axis_index("section"), lax.axis_index("ctx")
    core = lax.rem(me, 2)
    chip = lax.div(me, 2)

    def at(chip_index, core_index):
        return lax.rem(chip_index + 2 * chips, chips) * 2 + core_index

    right, left, sibling = at(chip + 1, core), at(chip - 1, core), at(chip, 1 - core)
    next_sec, prev_sec = lax.rem(sec + 1, sections), lax.rem(sec + sections - 1, sections)
    next_ctx, prev_ctx = lax.rem(me + 1, parts), lax.rem(me + parts - 1, parts)

    loads = [
        pltpu.make_async_copy(source, target, load_sem.at[slot])
        for slot, (source, target) in enumerate(
            [
                (filt.at[0], fil), (g_in, g_all), (d_in, d_all), (tw_cos_in, tw_cos), (tw_sin_in, tw_sin),
                (di_in, di_all), (gi_in, gi_all),
            ]
        )
    ]
    for load in loads:
        load.start()

    barrier = pltpu.get_barrier_semaphore()

    def greet(offset, carry):
        peer = lax.rem(me + offset, parts)
        pl.semaphore_signal(barrier, inc=1, device_id=(sec, peer), device_id_type=MESH)
        return carry

    lax.fori_loop(1, parts, greet, 0)
    pl.semaphore_signal(barrier, inc=1, device_id=(prev_sec, me), device_id_type=MESH)
    pl.semaphore_signal(barrier, inc=1, device_id=(prev_sec, prev_ctx), device_id_type=MESH)
    pl.semaphore_wait(barrier, parts + 1)

    relay = pltpu.make_async_remote_copy(
        act.at[0], rows_in, relay_send.at[0], relay_recv.at[0],
        device_id=(next_sec, me), device_id_type=MESH,
    )
    relay_halo = pltpu.make_async_remote_copy(
        act.at[0, pl.ds(tokens - HALO, HALO)], halo_in, relay_send.at[1], relay_recv.at[1],
        device_id=(next_sec, next_ctx), device_id_type=MESH,
    )

    hops_right = chips // 2
    hops_left = chips - 1 - hops_right
    sources = [
        in_w.at[0, :, pl.ds(width, width)], in_w.at[0, :, pl.ds(2 * width, width)],
        in_w.at[0, :, pl.ds(0, width)], out_w.at[0],
    ]

    def slot(kind, owner):
        return w.at[kind, pl.ds(pl.multiple_of(owner * depth, depth), depth)]

    def ring_copy(kind, source, owner, target):
        return pltpu.make_async_remote_copy(
            source, slot(kind, owner), ring_send.at[kind], ring_recv.at[kind, owner],
            device_id=(sec, target), device_id_type=MESH,
        )

    def arrived(kind, owner):
        pltpu.make_async_copy(slot(kind, owner), slot(kind, owner), ring_recv.at[kind, owner]).wait()

    def ring_start(kind):
        if hops_right:
            ring_copy(kind, sources[kind], me, right).start()
        if hops_left:
            ring_copy(kind, sources[kind], me, left).start()
        ring_copy(kind, sources[kind], me, sibling).start()
        pltpu.make_async_copy(sources[kind], slot(kind, me), own_sem.at[kind]).start()

    def ring_step(kind, step):
        if step <= hops_right:
            owner = at(chip - step, core)
            arrived(kind, owner)
            if step < hops_right:
                ring_copy(kind, slot(kind, owner), owner, right).start()
            ring_copy(kind, slot(kind, owner), owner, sibling).start()
        if step <= hops_left:
            owner = at(chip + step, core)
            arrived(kind, owner)
            if step < hops_left:
                ring_copy(kind, slot(kind, owner), owner, left).start()
            ring_copy(kind, slot(kind, owner), owner, sibling).start()

    def ring_finish(kind):
        pltpu.make_async_copy(sources[kind], slot(kind, me), own_sem.at[kind]).wait()

        def other(index, carry):
            arrived(kind, 2 * index + 1 - core)
            return carry

        lax.fori_loop(0, chips, other, 0)

    ring_start(0)
    relay.start()
    relay_halo.start()
    ring_start(1)

    def outer_rows(index, columns_high, columns_low):
        rows = pl.ds(pl.multiple_of(index * tile_o, tile_o), tile_o)
        value = dot(g_hi[rows, :], columns_high) + dot(g_lo[rows, :], columns_high)
        if columns_low is not None:
            value = value + dot(g_hi[rows, :], columns_low)
        outer[rows, :] = value

    tile_o = min(256, 2 * half_rows)
    tile_i = min(256, half_rows)

    def inner_rows(group, index):
        rows = pl.ds(index * tile_i, tile_i)
        lanes = pl.ds(group * block, block)
        real = outer[rows, lanes]
        imag = outer[pl.ds(half_rows + index * tile_i, tile_i), lanes]
        cos, sin = tw_cos[rows, :], tw_sin[rows, :]
        turned = jnp.concatenate([real * cos + imag * sin, imag * cos - real * sin], axis=1)
        high, low = split(turned)
        return dot3(high, low, d_hi[...], d_lo[...])

    groups = depth // HALF
    inner_tiles = half_rows // tile_i
    outer_tiles = 2 * half_rows // tile_o

    def filter_outer(first, count):
        pieces = []
        for group in range(groups):
            pieces.append(jnp.concatenate(
                [fil[pl.ds(group * HALF, HALF), pl.ds(n * block, block)] for n in range(parts)], axis=0
            ))
        high, low = split(jnp.concatenate(pieces, axis=1))
        for index in range(first, first + count):
            outer_rows(index, high, low)

    def filter_inner(group):
        for index in range(inner_tiles):
            spec[group, pl.ds(index * tile_i, tile_i), :] = inner_rows(group, index) * (1.0 / (parts * block))

    def norm(values, gain_row):
        values = values.astype(F32)
        scale = lax.rsqrt(jnp.mean(values * values, axis=-1, keepdims=True) + 1e-06)
        return values * scale * gain_row

    def norm_rows():
        relay.wait_recv()
        relay_halo.wait_recv()
        before = norm(halo_in[...], gain[...])
        normed[pl.ds(0, HALO), :] = jnp.where(me > 0, before, jnp.zeros_like(before)).astype(BF16)
        normed[pl.ds(HALO, tokens), :] = norm(rows_in[...], gain[...]).astype(BF16)

    def wait_loads(first, count):
        for load in loads[first : first + count]:
            load.wait()

    steps = max(hops_right, hops_left)
    def split_table(whole, high, low):
        high[...], low[...] = split(whole[...])

    between = [
        lambda: (wait_loads(0, 2), split_table(g_all, g_hi, g_lo)),
        lambda: filter_outer(0, outer_tiles // 2),
        lambda: filter_outer(outer_tiles // 2, outer_tiles - outer_tiles // 2),
        lambda: (wait_loads(2, 3), split_table(d_all, d_hi, d_lo), filter_inner(0)),
        lambda: [filter_inner(group) for group in range(1, groups)],
        norm_rows,
        lambda: (wait_loads(5, 2), split_table(di_all, di_hi, di_lo), split_table(gi_all, gi_hi, gi_lo)),
    ]
    for step in range(1, steps + 1):
        ring_step(0, step)
        ring_step(1, step)
        if between:
            between.pop(0)()
    for piece in between:
        piece()
    ring_start(2)
    ring_finish(0)
    ring_finish(1)

    def mixed(kind, column, place):
        columns = pl.ds(pl.multiple_of(column, tile), tile)
        feat[place] = dot(normed[...], w[kind, :, columns])
        base = (0 if kind == 2 else width * (kind + 1)) + column
        weights = [taps[i, :, pl.ds(pl.multiple_of(base, tile), tile)] for i in range(3)]
        value = weights[0] * feat[place, pl.ds(HALO, tokens), :]
        value = value + weights[1] * feat[place, pl.ds(HALO - 1, tokens), :]
        return value + weights[2] * feat[place, pl.ds(HALO - 2, tokens), :]

    tiles = width // tile
    per_tile = tile // depth

    def product_tile(index, carry):
        at_tile = lax.rem(lax.div(me, per_tile) + 1 + index, tiles)
        column = at_tile * tile
        value = (mixed(0, column, 0) * mixed(1, column, 1)).T.astype(BF16)
        first = pl.multiple_of(at_tile * per_tile, per_tile)
        prod[pl.ds(first, per_tile)] = value.reshape(per_tile, depth, tokens)

        def send(offset, inner):
            peer = first + offset

            @pl.when(peer != me)
            def _():
                pltpu.make_async_remote_copy(
                    prod.at[peer], chan.at[me], to_send, to_recv.at[me],
                    device_id=(sec, peer), device_id_type=MESH,
                ).start()

            return inner

        return lax.fori_loop(0, per_tile, send, carry)

    lax.fori_loop(0, tiles, product_tile, 0)
    chan[me] = prod[me]

    for step in range(1, steps + 1):
        ring_step(2, step)
    ring_start(3)
    ring_finish(2)

    def query_tile(index, carry):
        column = index * tile
        query[pl.ds(pl.multiple_of(column, tile), tile), :] = mixed(2, column, 0).T
        return carry

    lax.fori_loop(0, tiles, query_tile, 0)

    def to_here(offset, carry):
        peer = lax.rem(me + offset, parts)
        pltpu.make_async_copy(chan.at[peer], chan.at[peer], to_recv.at[peer]).wait()
        return carry

    lax.fori_loop(1, parts, to_here, 0)

    columns = jnp.concatenate(
        [chan[:, pl.ds(group * HALF, HALF), :].reshape(half_rows, block) for group in range(groups)], axis=1
    )
    for index in range(outer_tiles):
        outer_rows(index, columns, None)
    for group in range(groups):
        lanes = pl.ds(group * block, block)
        for index in range(inner_tiles):
            rows = pl.ds(index * tile_i, tile_i)
            data = inner_rows(group, index)
            real, imag = data[:, :block], data[:, block:]
            filter_real, filter_imag = spec[group, rows, pl.ds(0, block)], spec[group, rows, pl.ds(block, block)]
            product = jnp.concatenate(
                [real * filter_real - imag * filter_imag, real * filter_imag + imag * filter_real], axis=1
            )
            high, low = split(product)
            value = dot3(high, low, di_hi[...], di_lo[...])
            real, imag = value[:, :block], value[:, block:]
            cos, sin = tw_cos[rows, :], tw_sin[rows, :]
            high, low = split(real * cos - imag * sin)
            back_hi[rows, lanes], back_lo[rows, lanes] = high, low
            high, low = split(imag * cos + real * sin)
            below = pl.ds(half_rows + index * tile_i, tile_i)
            back_hi[below, lanes], back_lo[below, lanes] = high, low

    per_rows = tile_i // HALF
    back_tiles = half_rows // tile_i

    def conv_tile(index, carry):
        at_tile = lax.rem(lax.div(me, per_rows) + 1 + index, back_tiles)
        rows = pl.ds(pl.multiple_of(at_tile * tile_i, tile_i), tile_i)
        value = dot3(gi_hi[rows, :], gi_lo[rows, :], back_hi[...], back_lo[...]).astype(BF16)
        first = pl.multiple_of(at_tile * per_rows, per_rows)
        for group in range(groups):
            conv[pl.ds(first, per_rows), pl.ds(group * HALF, HALF), :] = value[
                :, group * block : (group + 1) * block
            ].reshape(per_rows, HALF, block)

        def send(offset, inner):
            peer = first + offset

            @pl.when(peer != me)
            def _():
                pltpu.make_async_remote_copy(
                    conv.at[peer], ret.at[me], back_send, back_recv.at[me],
                    device_id=(sec, peer), device_id_type=MESH,
                ).start()

            return inner

        return lax.fori_loop(0, per_rows, send, carry)

    lax.fori_loop(0, back_tiles, conv_tile, 0)
    ret[me] = conv[me]

    for step in range(1, steps + 1):
        ring_step(3, step)
    ring_finish(3)

    def back_here(offset, carry):
        peer = lax.rem(me + offset, parts)
        pltpu.make_async_copy(ret.at[peer], ret.at[peer], back_recv.at[peer]).wait()
        return carry

    lax.fori_loop(1, parts, back_here, 0)

    gated = (query[...] * ret[...].reshape(width, tokens).astype(F32)).astype(BF16)
    for index in range(tiles):
        span = pl.ds(index * tile, tile)
        mixing = dot(w[3, span, :], gated)
        out[0, :, span] = (rows_in[:, span].astype(F32) + mixing.T).astype(BF16)

    relay.wait_send()
    relay_halo.wait_send()
    sent = (hops_right + hops_left + chips) * depth
    for kind in range(4):
        all_sent = w.at[kind, pl.ds(0, sent)]
        pltpu.make_async_copy(all_sent, all_sent, ring_send.at[kind]).wait()
    others = prod.at[pl.ds(0, parts - 1)]
    pltpu.make_async_copy(others, others, to_send).wait()
    others = conv.at[pl.ds(0, parts - 1)]
    pltpu.make_async_copy(others, others, back_send).wait()


def shards(activations, norm_gain, in_weight, short_weight, long_filter, out_weight):
    sections, parts = lax.axis_size("section"), lax.axis_size("ctx")
    chips = parts // 2
    tokens, width = activations.shape[1:]
    depth = width // parts
    half_rows = parts * HALF
    lanes = depth // HALF * tokens
    tables = [jnp.asarray(table) for table in transform_tables(parts, tokens)]
    in_hbm = pl.BlockSpec(memory_space=pltpu.HBM)
    in_vmem = pl.BlockSpec(memory_space=pltpu.VMEM)
    tile = min(256, width)
    scratch = [
        pltpu.VMEM((4, width, width), BF16),
        pltpu.VMEM((tokens, width), BF16),
        pltpu.VMEM((HALO, width), BF16),
        pltpu.VMEM((HALO + tokens, width), BF16),
        pltpu.VMEM((2, HALO + tokens, tile), F32),
        pltpu.VMEM((parts, depth, tokens), BF16),
        pltpu.VMEM((parts, depth, tokens), BF16),
        pltpu.VMEM((width, tokens), F32),
        pltpu.VMEM((2 * half_rows, lanes), F32),
        pltpu.VMEM((depth // HALF, half_rows, 2 * tokens), F32),
        pltpu.VMEM((2 * half_rows, lanes), BF16),
        pltpu.VMEM((2 * half_rows, lanes), BF16),
        pltpu.VMEM((parts, depth, tokens), BF16),
        pltpu.VMEM((parts, depth, tokens), BF16),
        pltpu.VMEM(long_filter.shape[1:], F32),
        *[pltpu.VMEM(table.shape, F32) for table in tables],
        *[pltpu.VMEM(table.shape, BF16) for table in tables[:4] for _ in range(2)],
        pltpu.SemaphoreType.DMA((4,)),
        pltpu.SemaphoreType.DMA((4, parts)),
        pltpu.SemaphoreType.DMA((4,)),
        pltpu.SemaphoreType.DMA((2,)),
        pltpu.SemaphoreType.DMA((2,)),
        pltpu.SemaphoreType.DMA,
        pltpu.SemaphoreType.DMA((parts,)),
        pltpu.SemaphoreType.DMA,
        pltpu.SemaphoreType.DMA((parts,)),
        pltpu.SemaphoreType.DMA((len(tables) + 1,)),
    ]
    return pl.pallas_call(
        functools.partial(kernel, sections, chips, width, tokens),
        out_shape=jax.ShapeDtypeStruct(activations.shape, BF16),
        in_specs=[in_hbm, in_vmem, in_hbm, in_vmem] + [in_hbm] * (2 + len(tables)),
        out_specs=in_vmem,
        scratch_shapes=scratch,
        compiler_params=pltpu.CompilerParams(
            collective_id=0, has_side_effects=True, vmem_limit_bytes=63 * 1024 * 1024
        ),
    )(
        activations, norm_gain, in_weight, jnp.transpose(short_weight, (1, 0, 2)), long_filter,
        jnp.swapaxes(out_weight, 1, 2), *tables,
    )


def solution(mesh):
    return jax.shard_map(
        shards,
        mesh=mesh,
        in_specs=(
            P("section", "ctx", None),
            P("section", None),
            P("section", "ctx", None),
            P("section", None, None),
            P("section", "ctx", None),
            P("section", None, "ctx"),
        ),
        out_specs=P("section", "ctx", None),
        check_vma=False,
    )
```

```python
import functools
import math

import jax
import jax.numpy as jnp
import numpy as np
from jax import lax
from jax.experimental import pallas as pl
from jax.experimental.pallas import tpu as pltpu
from jax.sharding import PartitionSpec as P

MESH = pl.DeviceIdType.MESH
F32, BF16 = jnp.float32, jnp.bfloat16
HALO = 16
HALF = 16


def transform_tables(parts, block):
    points = parts * block
    k = np.arange(parts)[:, None] + 0.25
    outer = 2.0 * math.pi * k * np.arange(parts)[None, :] / parts
    eye = np.eye(HALF)
    forward = np.concatenate([np.kron(np.cos(outer), eye), np.kron(-np.sin(outer), eye)], axis=0)
    inner = 2.0 * math.pi * np.outer(np.arange(block), np.arange(block)) / block
    cos, sin = np.cos(inner), np.sin(inner)
    inner_forward = np.block([[cos, -sin], [sin, cos]])
    inner_inverse = np.block([[cos, sin], [-sin, cos]])
    twist = np.repeat(2.0 * math.pi * k * np.arange(block)[None, :] / points, HALF, axis=0)
    tables = (forward, forward.T, inner_forward, inner_inverse, np.cos(twist), np.sin(twist))
    return [np.asarray(table, np.float32) for table in tables]


def split(value):
    high = value.astype(BF16)
    return high, (value - high.astype(F32)).astype(BF16)


def dot(a, b):
    return jnp.dot(a, b, preferred_element_type=F32)


def dot3(a_high, a_low, b_high, b_low):
    return dot(a_high, b_high) + (dot(a_high, b_low) + dot(a_low, b_high))


def kernel(
    sections, chips, width, tokens,
    act, gain, in_w, taps, filt, out_w, g_in, gi_in, d_in, di_in, tw_cos_in, tw_sin_in,
    out,
    w, rows_in, halo_in, normed, feat, prod, chan, query, outer, spec, back_hi, back_lo, conv, ret,
    fil, g_all, gi_all, d_all, di_all, tw_cos, tw_sin, g_hi, g_lo, gi_hi, gi_lo, d_hi, d_lo, di_hi, di_lo,
    ring_send, ring_recv, pair_send, pair_recv, own_sem, relay_send, relay_recv, to_send, to_recv, back_send, back_recv,
    load_sem,
):
    parts = 2 * chips
    depth = width // parts
    block = tokens
    half_rows = parts * HALF
    tile = min(256, width)
    sec, me = lax.axis_index("section"), lax.axis_index("ctx")
    core = lax.rem(me, 2)
    chip = lax.div(me, 2)

    def at(chip_index, core_index):
        return lax.rem(chip_index + 2 * chips, chips) * 2 + core_index

    right, left, sibling = at(chip + 1, core), at(chip - 1, core), at(chip, 1 - core)
    next_sec, prev_sec = lax.rem(sec + 1, sections), lax.rem(sec + sections - 1, sections)
    next_ctx, prev_ctx = lax.rem(me + 1, parts), lax.rem(me + parts - 1, parts)

    loads = [
        pltpu.make_async_copy(source, target, load_sem.at[slot])
        for slot, (source, target) in enumerate(
            [
                (filt.at[0], fil), (g_in, g_all), (d_in, d_all), (tw_cos_in, tw_cos), (tw_sin_in, tw_sin),
                (di_in, di_all), (gi_in, gi_all),
            ]
        )
    ]
    for load in loads:
        load.start()

    barrier = pltpu.get_barrier_semaphore()
    for peer in (left, right, sibling):
        pl.semaphore_signal(barrier, inc=1, device_id=(sec, peer), device_id_type=MESH)
    pl.semaphore_signal(barrier, inc=1, device_id=(prev_sec, me), device_id_type=MESH)
    pl.semaphore_signal(barrier, inc=1, device_id=(prev_sec, prev_ctx), device_id_type=MESH)
    pl.semaphore_wait(barrier, 5)

    relay = pltpu.make_async_remote_copy(
        act.at[0], rows_in, relay_send.at[0], relay_recv.at[0],
        device_id=(next_sec, me), device_id_type=MESH,
    )
    relay_halo = pltpu.make_async_remote_copy(
        act.at[0, pl.ds(tokens - HALO, HALO)], halo_in, relay_send.at[1], relay_recv.at[1],
        device_id=(next_sec, next_ctx), device_id_type=MESH,
    )

    hops_right = chips // 2
    hops_left = chips - 1 - hops_right
    sources = [
        in_w.at[0, :, pl.ds(width, width)], in_w.at[0, :, pl.ds(2 * width, width)],
        in_w.at[0, :, pl.ds(0, width)], out_w.at[0],
    ]

    half = width // 2
    streams = [(0, 0, half), (1, 0, half), (0, half, half), (1, half, half), (2, 0, width), (3, 0, width)]
    key_value, late = (0, 1, 2, 3), (4, 5)

    def rows_of(owner):
        return pl.ds(pl.multiple_of(owner * depth, depth), depth)

    def ring_copy(stream, source, owner, target):
        kind, first, count = streams[stream]
        return pltpu.make_async_remote_copy(
            source, w.at[kind, rows_of(owner), pl.ds(first, count)],
            ring_send.at[stream], ring_recv.at[stream, owner],
            device_id=(sec, target), device_id_type=MESH,
        )

    def sibling_copy(kind, source, owner):
        return pltpu.make_async_remote_copy(
            source, w.at[kind, rows_of(owner)], pair_send.at[kind], pair_recv.at[kind, lax.div(owner, 2)],
            device_id=(sec, sibling), device_id_type=MESH,
        )

    def ring_start(group):
        for stream in group:
            kind, first, count = streams[stream]
            own = sources[kind].at[:, pl.ds(first, count)]
            if hops_right:
                ring_copy(stream, own, me, right).start()
            if hops_left:
                ring_copy(stream, own, me, left).start()
        for kind in sorted({streams[stream][0] for stream in group}):
            sibling_copy(kind, sources[kind], me).start()
            pltpu.make_async_copy(sources[kind], w.at[kind, rows_of(me)], own_sem.at[kind]).start()

    def ring_step(group, step):
        for stream in group:
            kind, first, count = streams[stream]
            for hops, owner, target in (
                (hops_right, at(chip - step, core), right), (hops_left, at(chip + step, core), left)
            ):
                if step > hops:
                    continue
                here = w.at[kind, rows_of(owner), pl.ds(first, count)]
                pltpu.make_async_copy(here, here, ring_recv.at[stream, owner]).wait()
                if step < hops:
                    ring_copy(stream, here, owner, target).start()
                if first + count == width:
                    sibling_copy(kind, w.at[kind, rows_of(owner)], owner).start()

    def ring_finish(kind):
        pltpu.make_async_copy(sources[kind], w.at[kind, rows_of(me)], own_sem.at[kind]).wait()

        def other(index, carry):
            here = w.at[kind, rows_of(2 * index + 1 - core)]
            pltpu.make_async_copy(here, here, pair_recv.at[kind, index]).wait()
            return carry

        lax.fori_loop(0, chips, other, 0)

    ring_start(key_value)
    relay.start()
    relay_halo.start()
    ring_start(late)

    def outer_rows(index, columns_high, columns_low):
        rows = pl.ds(pl.multiple_of(index * tile_o, tile_o), tile_o)
        value = dot(g_hi[rows, :], columns_high) + dot(g_lo[rows, :], columns_high)
        if columns_low is not None:
            value = value + dot(g_hi[rows, :], columns_low)
        outer[rows, :] = value

    tile_o = min(256, 2 * half_rows)
    tile_i = min(256, half_rows)

    def inner_rows(group, index):
        rows = pl.ds(index * tile_i, tile_i)
        lanes = pl.ds(group * block, block)
        real = outer[rows, lanes]
        imag = outer[pl.ds(half_rows + index * tile_i, tile_i), lanes]
        cos, sin = tw_cos[rows, :], tw_sin[rows, :]
        turned = jnp.concatenate([real * cos + imag * sin, imag * cos - real * sin], axis=1)
        high, low = split(turned)
        return dot3(high, low, d_hi[...], d_lo[...])

    groups = depth // HALF
    inner_tiles = half_rows // tile_i
    outer_tiles = 2 * half_rows // tile_o

    def filter_outer(first, count):
        pieces = []
        for group in range(groups):
            pieces.append(jnp.concatenate(
                [fil[pl.ds(group * HALF, HALF), pl.ds(n * block, block)] for n in range(parts)], axis=0
            ))
        high, low = split(jnp.concatenate(pieces, axis=1))
        for index in range(first, first + count):
            outer_rows(index, high, low)

    def filter_inner(group):
        for index in range(inner_tiles):
            spec[group, pl.ds(index * tile_i, tile_i), :] = inner_rows(group, index) * (1.0 / (parts * block))

    def norm(values, gain_row):
        values = values.astype(F32)
        scale = lax.rsqrt(jnp.mean(values * values, axis=-1, keepdims=True) + 1e-06)
        return values * scale * gain_row

    def norm_rows():
        relay.wait_recv()
        relay_halo.wait_recv()
        before = norm(halo_in[...], gain[...])
        normed[pl.ds(0, HALO), :] = jnp.where(me > 0, before, jnp.zeros_like(before)).astype(BF16)
        normed[pl.ds(HALO, tokens), :] = norm(rows_in[...], gain[...]).astype(BF16)

    def wait_loads(first, count):
        for load in loads[first : first + count]:
            load.wait()

    steps = max(hops_right, hops_left)
    def split_table(whole, high, low):
        high[...], low[...] = split(whole[...])

    between = [
        lambda: (wait_loads(0, 2), split_table(g_all, g_hi, g_lo)),
        lambda: filter_outer(0, outer_tiles // 2),
        lambda: filter_outer(outer_tiles // 2, outer_tiles - outer_tiles // 2),
        lambda: (wait_loads(2, 3), split_table(d_all, d_hi, d_lo), filter_inner(0)),
        lambda: [filter_inner(group) for group in range(1, groups)],
        norm_rows,
        lambda: (wait_loads(5, 2), split_table(di_all, di_hi, di_lo), split_table(gi_all, gi_hi, gi_lo)),
    ]
    late_done = 0
    for step in range(1, steps + 1):
        ring_step(key_value, step)
        if between:
            between.pop(0)()
        if step % 2 == 0:
            late_done += 1
            ring_step(late, late_done)
    for piece in between:
        piece()
    ring_finish(0)
    ring_finish(1)

    def mixed(kind, column, place):
        columns = pl.ds(pl.multiple_of(column, tile), tile)
        feat[place] = dot(normed[...], w[kind, :, columns])
        base = (0 if kind == 2 else width * (kind + 1)) + column
        weights = [taps[i, :, pl.ds(pl.multiple_of(base, tile), tile)] for i in range(3)]
        value = weights[0] * feat[place, pl.ds(HALO, tokens), :]
        value = value + weights[1] * feat[place, pl.ds(HALO - 1, tokens), :]
        return value + weights[2] * feat[place, pl.ds(HALO - 2, tokens), :]

    tiles = width // tile
    per_tile = tile // depth

    def product_tile(index, carry):
        at_tile = lax.rem(lax.div(me, per_tile) + 1 + index, tiles)
        column = at_tile * tile
        value = (mixed(0, column, 0) * mixed(1, column, 1)).T.astype(BF16)
        first = pl.multiple_of(at_tile * per_tile, per_tile)
        prod[pl.ds(first, per_tile)] = value.reshape(per_tile, depth, tokens)

        def send(offset, inner):
            peer = first + offset

            @pl.when(peer != me)
            def _():
                pltpu.make_async_remote_copy(
                    prod.at[peer], chan.at[me], to_send, to_recv.at[me],
                    device_id=(sec, peer), device_id_type=MESH,
                ).start()

            return inner

        return lax.fori_loop(0, per_tile, send, carry)

    lax.fori_loop(0, tiles, product_tile, 0)
    chan[me] = prod[me]

    while late_done < steps - 1:
        late_done += 1
        ring_step(late, late_done)

    def query_tile(index, carry):
        column = index * tile
        query[pl.ds(pl.multiple_of(column, tile), tile), :] = mixed(2, column, 0).T
        return carry

    def to_here(offset, carry):
        peer = lax.rem(me + offset, parts)
        pltpu.make_async_copy(chan.at[peer], chan.at[peer], to_recv.at[peer]).wait()
        return carry

    lax.fori_loop(1, parts, to_here, 0)

    columns = jnp.concatenate(
        [chan[:, pl.ds(group * HALF, HALF), :].reshape(half_rows, block) for group in range(groups)], axis=1
    )
    for index in range(outer_tiles):
        outer_rows(index, columns, None)
    for group in range(groups):
        lanes = pl.ds(group * block, block)
        for index in range(inner_tiles):
            rows = pl.ds(index * tile_i, tile_i)
            data = inner_rows(group, index)
            real, imag = data[:, :block], data[:, block:]
            filter_real, filter_imag = spec[group, rows, pl.ds(0, block)], spec[group, rows, pl.ds(block, block)]
            product = jnp.concatenate(
                [real * filter_real - imag * filter_imag, real * filter_imag + imag * filter_real], axis=1
            )
            high, low = split(product)
            value = dot3(high, low, di_hi[...], di_lo[...])
            real, imag = value[:, :block], value[:, block:]
            cos, sin = tw_cos[rows, :], tw_sin[rows, :]
            high, low = split(real * cos - imag * sin)
            back_hi[rows, lanes], back_lo[rows, lanes] = high, low
            high, low = split(imag * cos + real * sin)
            below = pl.ds(half_rows + index * tile_i, tile_i)
            back_hi[below, lanes], back_lo[below, lanes] = high, low

    per_rows = tile_i // HALF
    back_tiles = half_rows // tile_i

    def conv_tile(index, carry):
        at_tile = lax.rem(lax.div(me, per_rows) + 1 + index, back_tiles)
        rows = pl.ds(pl.multiple_of(at_tile * tile_i, tile_i), tile_i)
        value = dot3(gi_hi[rows, :], gi_lo[rows, :], back_hi[...], back_lo[...]).astype(BF16)
        first = pl.multiple_of(at_tile * per_rows, per_rows)
        for group in range(groups):
            conv[pl.ds(first, per_rows), pl.ds(group * HALF, HALF), :] = value[
                :, group * block : (group + 1) * block
            ].reshape(per_rows, HALF, block)

        def send(offset, inner):
            peer = first + offset

            @pl.when(peer != me)
            def _():
                pltpu.make_async_remote_copy(
                    conv.at[peer], ret.at[me], back_send, back_recv.at[me],
                    device_id=(sec, peer), device_id_type=MESH,
                ).start()

            return inner

        return lax.fori_loop(0, per_rows, send, carry)

    lax.fori_loop(0, back_tiles, conv_tile, 0)
    ret[me] = conv[me]

    while late_done < steps:
        late_done += 1
        ring_step(late, late_done)
    ring_finish(2)
    lax.fori_loop(0, tiles, query_tile, 0)
    ring_finish(3)

    def back_here(offset, carry):
        peer = lax.rem(me + offset, parts)
        pltpu.make_async_copy(ret.at[peer], ret.at[peer], back_recv.at[peer]).wait()
        return carry

    lax.fori_loop(1, parts, back_here, 0)

    gated = (query[...] * ret[...].reshape(width, tokens).astype(F32)).astype(BF16)
    for index in range(tiles):
        span = pl.ds(index * tile, tile)
        mixing = dot(w[3, span, :], gated)
        out[0, :, span] = (rows_in[:, span].astype(F32) + mixing.T).astype(BF16)

    relay.wait_send()
    relay_halo.wait_send()
    for stream in key_value + late:
        kind, first, count = streams[stream]
        all_sent = w.at[kind, pl.ds(0, (hops_right + hops_left) * depth), pl.ds(first, count)]
        pltpu.make_async_copy(all_sent, all_sent, ring_send.at[stream]).wait()
    for kind in range(4):
        all_sent = w.at[kind, pl.ds(0, chips * depth)]
        pltpu.make_async_copy(all_sent, all_sent, pair_send.at[kind]).wait()
    others = prod.at[pl.ds(0, parts - 1)]
    pltpu.make_async_copy(others, others, to_send).wait()
    others = conv.at[pl.ds(0, parts - 1)]
    pltpu.make_async_copy(others, others, back_send).wait()


def shards(activations, norm_gain, in_weight, short_weight, long_filter, out_weight):
    sections, parts = lax.axis_size("section"), lax.axis_size("ctx")
    chips = parts // 2
    tokens, width = activations.shape[1:]
    depth = width // parts
    half_rows = parts * HALF
    lanes = depth // HALF * tokens
    tables = [jnp.asarray(table) for table in transform_tables(parts, tokens)]
    in_hbm = pl.BlockSpec(memory_space=pltpu.HBM)
    in_vmem = pl.BlockSpec(memory_space=pltpu.VMEM)
    tile = min(256, width)
    scratch = [
        pltpu.VMEM((4, width, width), BF16),
        pltpu.VMEM((tokens, width), BF16),
        pltpu.VMEM((HALO, width), BF16),
        pltpu.VMEM((HALO + tokens, width), BF16),
        pltpu.VMEM((2, HALO + tokens, tile), F32),
        pltpu.VMEM((parts, depth, tokens), BF16),
        pltpu.VMEM((parts, depth, tokens), BF16),
        pltpu.VMEM((width, tokens), F32),
        pltpu.VMEM((2 * half_rows, lanes), F32),
        pltpu.VMEM((depth // HALF, half_rows, 2 * tokens), F32),
        pltpu.VMEM((2 * half_rows, lanes), BF16),
        pltpu.VMEM((2 * half_rows, lanes), BF16),
        pltpu.VMEM((parts, depth, tokens), BF16),
        pltpu.VMEM((parts, depth, tokens), BF16),
        pltpu.VMEM(long_filter.shape[1:], F32),
        *[pltpu.VMEM(table.shape, F32) for table in tables],
        *[pltpu.VMEM(table.shape, BF16) for table in tables[:4] for _ in range(2)],
        pltpu.SemaphoreType.DMA((6,)),
        pltpu.SemaphoreType.DMA((6, parts)),
        pltpu.SemaphoreType.DMA((4,)),
        pltpu.SemaphoreType.DMA((4, chips)),
        pltpu.SemaphoreType.DMA((4,)),
        pltpu.SemaphoreType.DMA((2,)),
        pltpu.SemaphoreType.DMA((2,)),
        pltpu.SemaphoreType.DMA,
        pltpu.SemaphoreType.DMA((parts,)),
        pltpu.SemaphoreType.DMA,
        pltpu.SemaphoreType.DMA((parts,)),
        pltpu.SemaphoreType.DMA((len(tables) + 1,)),
    ]
    return pl.pallas_call(
        functools.partial(kernel, sections, chips, width, tokens),
        out_shape=jax.ShapeDtypeStruct(activations.shape, BF16),
        in_specs=[in_hbm, in_vmem, in_hbm, in_vmem] + [in_hbm] * (2 + len(tables)),
        out_specs=in_vmem,
        scratch_shapes=scratch,
        compiler_params=pltpu.CompilerParams(
            collective_id=0, has_side_effects=True, vmem_limit_bytes=63 * 1024 * 1024
        ),
    )(
        activations, norm_gain, in_weight, jnp.transpose(short_weight, (1, 0, 2)), long_filter,
        jnp.swapaxes(out_weight, 1, 2), *tables,
    )


def solution(mesh):
    return jax.shard_map(
        shards,
        mesh=mesh,
        in_specs=(
            P("section", "ctx", None),
            P("section", None),
            P("section", "ctx", None),
            P("section", None, None),
            P("section", "ctx", None),
            P("section", None, "ctx"),
        ),
        out_specs=P("section", "ctx", None),
        check_vma=False,
    )
```

```python
import functools
import math

import jax
import jax.numpy as jnp
import numpy as np
from jax import lax
from jax.experimental import pallas as pl
from jax.experimental.pallas import tpu as pltpu
from jax.sharding import PartitionSpec as P

MESH = pl.DeviceIdType.MESH
F32, BF16 = jnp.float32, jnp.bfloat16
HALO = 16
FEW = 8
PAIR = 2 * FEW


def transform_tables(parts, block):
    points = parts * block
    k = np.arange(parts)[:, None] + 0.25
    outer = 2.0 * math.pi * k * np.arange(parts)[None, :] / parts
    eye = np.eye(FEW)
    forward = np.concatenate([np.kron(np.cos(outer), eye), np.kron(-np.sin(outer), eye)], axis=0)
    inner = 2.0 * math.pi * np.outer(np.arange(block), np.arange(block)) / block
    cos, sin = np.cos(inner), np.sin(inner)
    inner_forward = np.block([[cos, -sin], [sin, cos]])
    inner_inverse = np.block([[cos, sin], [-sin, cos]])
    twist = np.repeat(2.0 * math.pi * k * np.arange(block)[None, :] / points, FEW, axis=0)
    tables = (forward, forward.T, inner_forward, inner_inverse, np.cos(twist), np.sin(twist))
    return [np.asarray(table, np.float32) for table in tables]


def split(value):
    high = value.astype(BF16)
    return high, (value - high.astype(F32)).astype(BF16)


def dot(a, b):
    return jnp.dot(a, b, preferred_element_type=F32)


def dot3(a_high, a_low, b_high, b_low):
    return dot(a_high, b_high) + (dot(a_high, b_low) + dot(a_low, b_high))


def kernel(
    sections, chips, width, tokens,
    act, gain, in_w, taps, filt, out_w, g_in, gi_in, d_in, di_in, tw_cos_in, tw_sin_in,
    out,
    w, rows_in, halo_in, normed, feat, prod, chan, query, outer, spec, back_hi, back_lo, conv, ret, gated,
    fil, g_all, gi_all, d_all, di_all, tw_cos, tw_sin, g_hi, g_lo, gi_hi, gi_lo, d_hi, d_lo, di_hi, di_lo,
    ring_send, ring_recv, pair_send, pair_recv, own_sem, relay_send, relay_recv, to_send, to_recv, back_send, back_recv,
    load_sem,
):
    parts = 2 * chips
    depth = width // parts
    block = tokens
    rows_k = parts * FEW
    pairs = depth // PAIR
    tile = min(256, width)
    sec, me = lax.axis_index("section"), lax.axis_index("ctx")
    core = lax.rem(me, 2)
    chip = lax.div(me, 2)

    def at(chip_index, core_index):
        return lax.rem(chip_index + 2 * chips, chips) * 2 + core_index

    right, left, sibling = at(chip + 1, core), at(chip - 1, core), at(chip, 1 - core)
    next_sec, prev_sec = lax.rem(sec + 1, sections), lax.rem(sec + sections - 1, sections)
    next_ctx, prev_ctx = lax.rem(me + 1, parts), lax.rem(me + parts - 1, parts)

    loads = [
        pltpu.make_async_copy(source, target, load_sem.at[slot])
        for slot, (source, target) in enumerate(
            [
                (filt.at[0], fil), (g_in, g_all), (d_in, d_all), (tw_cos_in, tw_cos), (tw_sin_in, tw_sin),
                (di_in, di_all), (gi_in, gi_all),
            ]
        )
    ]
    for load in loads:
        load.start()

    barrier = pltpu.get_barrier_semaphore()
    for peer in (left, right, sibling):
        pl.semaphore_signal(barrier, inc=1, device_id=(sec, peer), device_id_type=MESH)
    pl.semaphore_signal(barrier, inc=1, device_id=(prev_sec, me), device_id_type=MESH)
    pl.semaphore_signal(barrier, inc=1, device_id=(prev_sec, prev_ctx), device_id_type=MESH)
    pl.semaphore_wait(barrier, 5)

    relay = pltpu.make_async_remote_copy(
        act.at[0], rows_in, relay_send.at[0], relay_recv.at[0],
        device_id=(next_sec, me), device_id_type=MESH,
    )
    relay_halo = pltpu.make_async_remote_copy(
        act.at[0, pl.ds(tokens - HALO, HALO)], halo_in, relay_send.at[1], relay_recv.at[1],
        device_id=(next_sec, next_ctx), device_id_type=MESH,
    )

    hops = [(chips // 2, chips - 1 - chips // 2), (chips - 1 - chips // 2, chips // 2)]
    sources = [
        in_w.at[0, :, pl.ds(width, width)], in_w.at[0, :, pl.ds(2 * width, width)],
        in_w.at[0, :, pl.ds(0, width)], out_w.at[0],
    ]

    streams = [(0, 0, width), (1, 0, width), (2, 0, width), (3, 0, width)]
    key_value, late = (0, 1), (2, 3)

    def rows_of(owner):
        return pl.ds(pl.multiple_of(owner * depth, depth), depth)

    def ring_copy(stream, source, owner, target):
        kind, first, count = streams[stream]
        return pltpu.make_async_remote_copy(
            source, w.at[kind, rows_of(owner), pl.ds(first, count)],
            ring_send.at[stream], ring_recv.at[stream, owner],
            device_id=(sec, target), device_id_type=MESH,
        )

    def sibling_copy(kind, source, owner):
        return pltpu.make_async_remote_copy(
            source, w.at[kind, rows_of(owner)], pair_send.at[kind], pair_recv.at[kind, lax.div(owner, 2)],
            device_id=(sec, sibling), device_id_type=MESH,
        )

    def ring_start(group):
        for stream in group:
            kind, first, count = streams[stream]
            own = sources[kind].at[:, pl.ds(first, count)]
            for count, target in zip(hops[stream % 2], (right, left)):
                if count:
                    ring_copy(stream, own, me, target).start()
        for kind in sorted({streams[stream][0] for stream in group}):
            sibling_copy(kind, sources[kind], me).start()
            pltpu.make_async_copy(sources[kind], w.at[kind, rows_of(me)], own_sem.at[kind]).start()

    def ring_step(group, step):
        for stream in group:
            kind, first, count = streams[stream]
            ways = ((at(chip - step, core), right), (at(chip + step, core), left))
            for far, (owner, target) in zip(hops[stream % 2], ways):
                if step > far:
                    continue
                here = w.at[kind, rows_of(owner), pl.ds(first, count)]
                pltpu.make_async_copy(here, here, ring_recv.at[stream, owner]).wait()
                if step < far:
                    ring_copy(stream, here, owner, target).start()
                if first + count == width:
                    sibling_copy(kind, w.at[kind, rows_of(owner)], owner).start()

    def ring_finish(kind):
        pltpu.make_async_copy(sources[kind], w.at[kind, rows_of(me)], own_sem.at[kind]).wait()

        def other(index, carry):
            here = w.at[kind, rows_of(2 * index + 1 - core)]
            pltpu.make_async_copy(here, here, pair_recv.at[kind, index]).wait()
            return carry

        lax.fori_loop(0, chips, other, 0)

    ring_start(key_value)
    relay.start()
    relay_halo.start()
    ring_start(late)

    def outer_rows(pair, columns_high, columns_low):
        lanes = pl.ds(2 * block * pair, 2 * block)
        for index in range(2):
            rows = pl.ds(index * rows_k, rows_k)
            value = dot(g_hi[rows, :], columns_high) + dot(g_lo[rows, :], columns_high)
            if columns_low is not None:
                value = value + dot(g_hi[rows, :], columns_low)
            outer[rows, lanes] = value

    def inner_rows(group):
        lanes = pl.ds(group * block, block)
        real, imag = outer[pl.ds(0, rows_k), lanes], outer[pl.ds(rows_k, rows_k), lanes]
        cos, sin = tw_cos[...], tw_sin[...]
        turned = jnp.concatenate([real * cos + imag * sin, imag * cos - real * sin], axis=1)
        high, low = split(turned)
        return dot3(high, low, d_hi[...], d_lo[...])

    def filter_outer(pair):
        columns = [
            jnp.concatenate(
                [fil[pl.ds(group * FEW, FEW), pl.ds(n * block, block)] for n in range(parts)], axis=0
            )
            for group in (2 * pair, 2 * pair + 1)
        ]
        high, low = split(jnp.concatenate(columns, axis=1))
        outer_rows(pair, high, low)

    def filter_inner(group):
        spec[group] = inner_rows(group) * (1.0 / (parts * block))

    def norm(values, gain_row):
        values = values.astype(F32)
        scale = lax.rsqrt(jnp.mean(values * values, axis=-1, keepdims=True) + 1e-06)
        return values * scale * gain_row

    def norm_rows():
        relay.wait_recv()
        relay_halo.wait_recv()
        before = norm(halo_in[...], gain[...])
        normed[pl.ds(0, HALO), :] = jnp.where(me > 0, before, jnp.zeros_like(before)).astype(BF16)
        normed[pl.ds(HALO, tokens), :] = norm(rows_in[...], gain[...]).astype(BF16)

    def wait_loads(first, count):
        for load in loads[first : first + count]:
            load.wait()

    steps = chips // 2
    def split_table(whole, high, low):
        high[...], low[...] = split(whole[...])

    between = [
        lambda: (wait_loads(0, 2), split_table(g_all, g_hi, g_lo)),
        lambda: [filter_outer(pair) for pair in range(pairs)],
        lambda: (wait_loads(2, 3), split_table(d_all, d_hi, d_lo), filter_inner(0), filter_inner(1)),
        lambda: [filter_inner(group) for group in range(2, 2 * pairs)],
        norm_rows,
        lambda: (wait_loads(5, 2), split_table(di_all, di_hi, di_lo), split_table(gi_all, gi_hi, gi_lo)),
    ]
    late_done = 0
    for step in range(1, steps + 1):
        ring_step(key_value, step)
        if between:
            between.pop(0)()
        if step >= 2:
            late_done += 1
            ring_step(late, late_done)
    for piece in between:
        piece()
    ring_finish(0)
    ring_finish(1)

    def mixed(kind, column, place):
        columns = pl.ds(pl.multiple_of(column, tile), tile)
        feat[place] = dot(normed[...], w[kind, :, columns])
        base = (0 if kind == 2 else width * (kind + 1)) + column
        weights = [taps[i, :, pl.ds(pl.multiple_of(base, tile), tile)] for i in range(3)]
        value = weights[0] * feat[place, pl.ds(HALO, tokens), :]
        value = value + weights[1] * feat[place, pl.ds(HALO - 1, tokens), :]
        return value + weights[2] * feat[place, pl.ds(HALO - 2, tokens), :]

    tiles = width // tile
    per_tile = tile // depth

    def product_tile(index, carry):
        at_tile = lax.rem(lax.div(me, per_tile) + 1 + index, tiles)
        column = at_tile * tile
        value = (mixed(0, column, 0) * mixed(1, column, 1)).T.astype(BF16)
        first = pl.multiple_of(at_tile * per_tile, per_tile)
        prod[pl.ds(first, per_tile)] = value.reshape(per_tile, depth, tokens)

        lax.fori_loop(0, per_tile, lambda offset, inner: send(0, first + offset, inner), 0)
        return carry

    def over(source, target, send_sem, recv_sem):
        def send(pair, peer, carry):
            channels = pl.ds(pair * PAIR, PAIR)

            @pl.when(peer != me)
            def _():
                pltpu.make_async_remote_copy(
                    source.at[peer, channels], target.at[me, channels], send_sem.at[pair], recv_sem.at[pair, me],
                    device_id=(sec, peer), device_id_type=MESH,
                ).start()

            return carry

        def here(pair):
            def one(offset, carry):
                peer = lax.rem(me + offset, parts)
                landed = target.at[peer, pl.ds(pair * PAIR, PAIR)]
                pltpu.make_async_copy(landed, landed, recv_sem.at[pair, peer]).wait()
                return carry

            lax.fori_loop(1, parts, one, 0)

        def left_here():
            for pair in range(pairs):
                others = source.at[pl.ds(0, parts - 1), pl.ds(0, PAIR)]
                pltpu.make_async_copy(others, others, send_sem.at[pair]).wait()

        return send, here, left_here

    send, product_here, product_left = over(prod, chan, to_send, to_recv)
    send_back, conv_here, conv_left = over(conv, ret, back_send, back_recv)

    def to_all(send_one, pair):
        lax.fori_loop(1, parts, lambda offset, carry: send_one(pair, lax.rem(me + offset, parts), carry), 0)

    lax.fori_loop(0, tiles, product_tile, 0)
    for pair in range(1, pairs):
        to_all(send, pair)
    chan[me] = prod[me]

    def late_step():
        nonlocal late_done
        if late_done < steps:
            late_done += 1
            ring_step(late, late_done)

    late_step()

    def convolve(pair):
        data = chan[:, pl.ds(pair * PAIR, PAIR), :].astype(F32)
        columns = jnp.concatenate(
            [data[:, :FEW].reshape(rows_k, block), data[:, FEW:].reshape(rows_k, block)], axis=1
        )
        outer_rows(pair, columns.astype(BF16), None)
        for group in (2 * pair, 2 * pair + 1):
            lanes = pl.ds(group * block, block)
            data = inner_rows(group)
            real, imag = data[:, :block], data[:, block:]
            filter_real, filter_imag = spec[group, :, pl.ds(0, block)], spec[group, :, pl.ds(block, block)]
            points = jnp.concatenate(
                [real * filter_real - imag * filter_imag, real * filter_imag + imag * filter_real], axis=1
            )
            high, low = split(points)
            value = dot3(high, low, di_hi[...], di_lo[...])
            real, imag = value[:, :block], value[:, block:]
            cos, sin = tw_cos[...], tw_sin[...]
            above, below = pl.ds(0, rows_k), pl.ds(rows_k, rows_k)
            back_hi[above, lanes], back_lo[above, lanes] = split(real * cos - imag * sin)
            back_hi[below, lanes], back_lo[below, lanes] = split(imag * cos + real * sin)
        lanes = pl.ds(2 * block * pair, 2 * block)
        value = dot3(gi_hi[...], gi_lo[...], back_hi[:, lanes], back_lo[:, lanes])
        whole = jnp.concatenate(
            [value[:, :block].reshape(parts, FEW, block), value[:, block:].reshape(parts, FEW, block)], axis=1
        )
        conv[:, pl.ds(pair * PAIR, PAIR), :] = whole.astype(BF16)

    for pair in range(pairs):
        product_here(pair)
        convolve(pair)
        to_all(send_back, pair)
        late_step()
    ret[me] = conv[me]
    while late_done < steps:
        late_step()

    def query_tile(index, carry):
        value = mixed(2, index * tile, 0).T
        query[pl.ds(pl.multiple_of(index * per_tile, per_tile), per_tile)] = value.reshape(per_tile, depth, tokens)
        return carry

    ring_finish(2)
    lax.fori_loop(0, tiles, query_tile, 0)
    ring_finish(3)

    for pair in range(pairs):
        conv_here(pair)
        channels = pl.ds(pair * PAIR, PAIR)
        gated[:, channels, :] = (query[:, channels, :] * ret[:, channels, :].astype(F32)).astype(BF16)
    gates = gated[...].reshape(width, tokens)
    for index in range(tiles):
        span = pl.ds(index * tile, tile)
        mixing = dot(w[3, span, :], gates)
        out[0, :, span] = (rows_in[:, span].astype(F32) + mixing.T).astype(BF16)

    relay.wait_send()
    relay_halo.wait_send()
    for stream in key_value + late:
        kind, first, count = streams[stream]
        all_sent = w.at[kind, pl.ds(0, (chips - 1) * depth), pl.ds(first, count)]
        pltpu.make_async_copy(all_sent, all_sent, ring_send.at[stream]).wait()
    for kind in range(4):
        all_sent = w.at[kind, pl.ds(0, chips * depth)]
        pltpu.make_async_copy(all_sent, all_sent, pair_send.at[kind]).wait()
    product_left()
    conv_left()


def shards(activations, norm_gain, in_weight, short_weight, long_filter, out_weight):
    sections, parts = lax.axis_size("section"), lax.axis_size("ctx")
    chips = parts // 2
    tokens, width = activations.shape[1:]
    depth = width // parts
    rows_k = parts * FEW
    groups, pairs = depth // FEW, depth // PAIR
    tables = [jnp.asarray(table) for table in transform_tables(parts, tokens)]
    in_hbm = pl.BlockSpec(memory_space=pltpu.HBM)
    in_vmem = pl.BlockSpec(memory_space=pltpu.VMEM)
    tile = min(256, width)
    scratch = [
        pltpu.VMEM((4, width, width), BF16),
        pltpu.VMEM((tokens, width), BF16),
        pltpu.VMEM((HALO, width), BF16),
        pltpu.VMEM((HALO + tokens, width), BF16),
        pltpu.VMEM((2, HALO + tokens, tile), F32),
        pltpu.VMEM((parts, depth, tokens), BF16),
        pltpu.VMEM((parts, depth, tokens), BF16),
        pltpu.VMEM((parts, depth, tokens), F32),
        pltpu.VMEM((2 * rows_k, groups * tokens), F32),
        pltpu.VMEM((groups, rows_k, 2 * tokens), F32),
        pltpu.VMEM((2 * rows_k, groups * tokens), BF16),
        pltpu.VMEM((2 * rows_k, groups * tokens), BF16),
        pltpu.VMEM((parts, depth, tokens), BF16),
        pltpu.VMEM((parts, depth, tokens), BF16),
        pltpu.VMEM((parts, depth, tokens), BF16),
        pltpu.VMEM(long_filter.shape[1:], F32),
        *[pltpu.VMEM(table.shape, F32) for table in tables],
        *[pltpu.VMEM(table.shape, BF16) for table in tables[:4] for _ in range(2)],
        pltpu.SemaphoreType.DMA((4,)),
        pltpu.SemaphoreType.DMA((4, parts)),
        pltpu.SemaphoreType.DMA((4,)),
        pltpu.SemaphoreType.DMA((4, chips)),
        pltpu.SemaphoreType.DMA((4,)),
        pltpu.SemaphoreType.DMA((2,)),
        pltpu.SemaphoreType.DMA((2,)),
        pltpu.SemaphoreType.DMA((pairs,)),
        pltpu.SemaphoreType.DMA((pairs, parts)),
        pltpu.SemaphoreType.DMA((pairs,)),
        pltpu.SemaphoreType.DMA((pairs, parts)),
        pltpu.SemaphoreType.DMA((len(tables) + 1,)),
    ]
    return pl.pallas_call(
        functools.partial(kernel, sections, chips, width, tokens),
        out_shape=pltpu.VMEM(activations.shape, BF16),
        in_specs=[in_hbm, in_vmem, in_hbm, in_vmem] + [in_hbm] * (2 + len(tables)),
        out_specs=in_vmem,
        scratch_shapes=scratch,
        compiler_params=pltpu.CompilerParams(
            collective_id=0, has_side_effects=True, vmem_limit_bytes=63 * 1024 * 1024
        ),
    )(
        activations, norm_gain, in_weight, jnp.transpose(short_weight, (1, 0, 2)), long_filter,
        jnp.swapaxes(out_weight, 1, 2), *tables,
    )


def solution(mesh):
    return jax.shard_map(
        shards,
        mesh=mesh,
        in_specs=(
            P("section", "ctx", None),
            P("section", None),
            P("section", "ctx", None),
            P("section", None, None),
            P("section", "ctx", None),
            P("section", None, "ctx"),
        ),
        out_specs=P("section", "ctx", None),
        check_vma=False,
    )
```

```python
import functools
import math

import jax
import jax.numpy as jnp
import numpy as np
from jax import lax
from jax.experimental import pallas as pl
from jax.experimental.pallas import tpu as pltpu
from jax.sharding import PartitionSpec as P

MESH = pl.DeviceIdType.MESH
F32, BF16 = jnp.float32, jnp.bfloat16
HALO = 16
FEW = 8
PAIR = 2 * FEW


def transform_tables(parts, block):
    points = parts * block
    k = np.arange(parts)[:, None] + 0.25
    outer = 2.0 * math.pi * k * np.arange(parts)[None, :] / parts
    eye = np.eye(FEW)
    forward = np.concatenate([np.kron(np.cos(outer), eye), np.kron(-np.sin(outer), eye)], axis=0)
    inner = 2.0 * math.pi * np.outer(np.arange(block), np.arange(block)) / block
    cos, sin = np.cos(inner), np.sin(inner)
    inner_forward = np.block([[cos, -sin], [sin, cos]])
    inner_inverse = np.block([[cos, sin], [-sin, cos]])
    twist = np.repeat(2.0 * math.pi * k * np.arange(block)[None, :] / points, FEW, axis=0)
    tables = (forward, forward.T, inner_forward, inner_inverse, np.cos(twist), np.sin(twist))
    return [np.asarray(table, np.float32) for table in tables]


def split(value):
    high = value.astype(BF16)
    return high, (value - high.astype(F32)).astype(BF16)


def dot(a, b):
    return jnp.dot(a, b, preferred_element_type=F32)


def dot3(a_high, a_low, b_high, b_low):
    return dot(a_high, b_high) + (dot(a_high, b_low) + dot(a_low, b_high))


def kernel(
    sections, chips, width, tokens,
    act, gain, in_w, taps, filt, out_w, g_in, gi_in, d_in, di_in, tw_cos_in, tw_sin_in,
    out,
    w, rows_in, halo_in, normed, feat, prod, chan, query, outer, spec, back_hi, back_lo, conv, ret,
    fil, g_all, gi_all, d_all, di_all, tw_cos, tw_sin, g_hi, g_lo, gi_hi, gi_lo, d_hi, d_lo, di_hi, di_lo,
    ring_send, ring_recv, pair_send, pair_recv, own_sem, relay_send, relay_recv, to_send, to_recv, back_send, back_recv,
    load_sem,
):
    parts = 2 * chips
    depth = width // parts
    block = tokens
    rows_k = parts * FEW
    pairs = depth // PAIR
    tile = min(256, width)
    sec, me = lax.axis_index("section"), lax.axis_index("ctx")
    core = lax.rem(me, 2)
    chip = lax.div(me, 2)

    def at(chip_index, core_index):
        return lax.rem(chip_index + 2 * chips, chips) * 2 + core_index

    right, left, sibling = at(chip + 1, core), at(chip - 1, core), at(chip, 1 - core)
    next_sec, prev_sec = lax.rem(sec + 1, sections), lax.rem(sec + sections - 1, sections)
    next_ctx, prev_ctx = lax.rem(me + 1, parts), lax.rem(me + parts - 1, parts)

    loads = [
        pltpu.make_async_copy(source, target, load_sem.at[slot])
        for slot, (source, target) in enumerate(
            [
                (filt.at[0], fil), (g_in, g_all), (d_in, d_all), (tw_cos_in, tw_cos), (tw_sin_in, tw_sin),
                (di_in, di_all), (gi_in, gi_all),
            ]
        )
    ]
    for load in loads:
        load.start()

    barrier = pltpu.get_barrier_semaphore()
    for peer in (left, right, sibling):
        pl.semaphore_signal(barrier, inc=1, device_id=(sec, peer), device_id_type=MESH)
    pl.semaphore_signal(barrier, inc=1, device_id=(prev_sec, me), device_id_type=MESH)
    pl.semaphore_signal(barrier, inc=1, device_id=(prev_sec, prev_ctx), device_id_type=MESH)
    pl.semaphore_wait(barrier, 5)

    relay = pltpu.make_async_remote_copy(
        act.at[0], rows_in, relay_send.at[0], relay_recv.at[0],
        device_id=(next_sec, me), device_id_type=MESH,
    )
    relay_halo = pltpu.make_async_remote_copy(
        act.at[0, pl.ds(tokens - HALO, HALO)], halo_in, relay_send.at[1], relay_recv.at[1],
        device_id=(next_sec, next_ctx), device_id_type=MESH,
    )

    hops = [(chips // 2, chips - 1 - chips // 2), (chips - 1 - chips // 2, chips // 2)]
    sources = [
        in_w.at[0, :, pl.ds(width, width)], in_w.at[0, :, pl.ds(2 * width, width)],
        in_w.at[0, :, pl.ds(0, width)], out_w.at[0],
    ]

    streams = [(0, 0, width), (1, 0, width), (2, 0, width), (3, 0, width)]
    key_value, late = (0, 1), (2, 3)

    def rows_of(owner):
        return pl.ds(pl.multiple_of(owner * depth, depth), depth)

    def ring_copy(stream, source, owner, target):
        kind, first, count = streams[stream]
        return pltpu.make_async_remote_copy(
            source, w.at[kind, rows_of(owner), pl.ds(first, count)],
            ring_send.at[stream], ring_recv.at[stream, owner],
            device_id=(sec, target), device_id_type=MESH,
        )

    def sibling_copy(kind, source, owner):
        return pltpu.make_async_remote_copy(
            source, w.at[kind, rows_of(owner)], pair_send.at[kind], pair_recv.at[kind, lax.div(owner, 2)],
            device_id=(sec, sibling), device_id_type=MESH,
        )

    def ring_start(group):
        for stream in group:
            kind, first, count = streams[stream]
            own = sources[kind].at[:, pl.ds(first, count)]
            for count, target in zip(hops[stream % 2], (right, left)):
                if count:
                    ring_copy(stream, own, me, target).start()
        for kind in sorted({streams[stream][0] for stream in group}):
            sibling_copy(kind, sources[kind], me).start()
            pltpu.make_async_copy(sources[kind], w.at[kind, rows_of(me)], own_sem.at[kind]).start()

    def ring_step(group, step):
        for stream in group:
            kind, first, count = streams[stream]
            ways = ((at(chip - step, core), right), (at(chip + step, core), left))
            for far, (owner, target) in zip(hops[stream % 2], ways):
                if step > far:
                    continue
                here = w.at[kind, rows_of(owner), pl.ds(first, count)]
                pltpu.make_async_copy(here, here, ring_recv.at[stream, owner]).wait()
                if step < far:
                    ring_copy(stream, here, owner, target).start()
                if first + count == width:
                    sibling_copy(kind, w.at[kind, rows_of(owner)], owner).start()

    def ring_finish(kind):
        pltpu.make_async_copy(sources[kind], w.at[kind, rows_of(me)], own_sem.at[kind]).wait()

        def other(index, carry):
            here = w.at[kind, rows_of(2 * index + 1 - core)]
            pltpu.make_async_copy(here, here, pair_recv.at[kind, index]).wait()
            return carry

        lax.fori_loop(0, chips, other, 0)

    ring_start(key_value)
    relay.start()
    relay_halo.start()
    ring_start(late)

    def outer_rows(pair, columns_high, columns_low):
        lanes = pl.ds(2 * block * pair, 2 * block)
        for index in range(2):
            rows = pl.ds(index * rows_k, rows_k)
            value = dot(g_hi[rows, :], columns_high) + dot(g_lo[rows, :], columns_high)
            if columns_low is not None:
                value = value + dot(g_hi[rows, :], columns_low)
            outer[rows, lanes] = value

    def inner_rows(group):
        lanes = pl.ds(group * block, block)
        real, imag = outer[pl.ds(0, rows_k), lanes], outer[pl.ds(rows_k, rows_k), lanes]
        cos, sin = tw_cos[...], tw_sin[...]
        turned = jnp.concatenate([real * cos + imag * sin, imag * cos - real * sin], axis=1)
        high, low = split(turned)
        return dot3(high, low, d_hi[...], d_lo[...])

    def filter_outer(pair):
        columns = [
            jnp.concatenate(
                [fil[pl.ds(group * FEW, FEW), pl.ds(n * block, block)] for n in range(parts)], axis=0
            )
            for group in (2 * pair, 2 * pair + 1)
        ]
        high, low = split(jnp.concatenate(columns, axis=1))
        outer_rows(pair, high, low)

    def filter_inner(group):
        spec[group] = inner_rows(group) * (1.0 / (parts * block))

    def norm(values, gain_row):
        values = values.astype(F32)
        scale = lax.rsqrt(jnp.mean(values * values, axis=-1, keepdims=True) + 1e-06)
        return values * scale * gain_row

    def norm_rows():
        relay.wait_recv()
        relay_halo.wait_recv()
        before = norm(halo_in[...], gain[...])
        normed[pl.ds(0, HALO), :] = jnp.where(me > 0, before, jnp.zeros_like(before)).astype(BF16)
        normed[pl.ds(HALO, tokens), :] = norm(rows_in[...], gain[...]).astype(BF16)

    def wait_loads(first, count):
        for load in loads[first : first + count]:
            load.wait()

    steps = chips // 2
    def split_table(whole, high, low):
        high[...], low[...] = split(whole[...])

    between = [
        lambda: (wait_loads(0, 2), split_table(g_all, g_hi, g_lo)),
        lambda: [filter_outer(pair) for pair in range(pairs)],
        lambda: (wait_loads(2, 3), split_table(d_all, d_hi, d_lo), filter_inner(0), filter_inner(1)),
        lambda: [filter_inner(group) for group in range(2, 2 * pairs)],
        norm_rows,
        lambda: (wait_loads(5, 2), split_table(di_all, di_hi, di_lo), split_table(gi_all, gi_hi, gi_lo)),
    ]
    late_done = 0
    for step in range(1, steps + 1):
        ring_step(key_value, step)
        if between:
            between.pop(0)()
        if 2 <= step < steps:
            late_done += 1
            ring_step(late, late_done)
    for piece in between:
        piece()
    def mixed(kind, column, place):
        columns = pl.ds(pl.multiple_of(column, tile), tile)
        feat[place] = dot(normed[...], w[kind, :, columns])
        base = (0 if kind == 2 else width * (kind + 1)) + column
        weights = [taps[i, :, pl.ds(pl.multiple_of(base, tile), tile)] for i in range(3)]
        value = weights[0] * feat[place, pl.ds(HALO, tokens), :]
        value = value + weights[1] * feat[place, pl.ds(HALO - 1, tokens), :]
        return value + weights[2] * feat[place, pl.ds(HALO - 2, tokens), :]

    tiles = width // tile
    per_tile = tile // depth

    turns = [2, 1, 3, 0] if tiles == 4 else [*range(1, tiles), 0]

    def quarter(turn):
        return lax.rem(lax.div(me, per_tile) + turn, tiles)

    def product_tile(index, carry):
        at_tile = lax.rem(lax.div(me, per_tile) + 2 + index, tiles)
        column = at_tile * tile
        value = (mixed(0, column, 0) * mixed(1, column, 1)).T.astype(BF16)
        first = pl.multiple_of(at_tile * per_tile, per_tile)
        prod[pl.ds(first, per_tile)] = value.reshape(per_tile, depth, tokens)

        lax.fori_loop(0, per_tile, lambda offset, inner: send(0, first + offset, inner), 0)
        return carry

    def over(source, target, send_sem, recv_sem):
        def send(pair, peer, carry):
            channels = pl.ds(pair * PAIR, PAIR)

            @pl.when(peer != me)
            def _():
                pltpu.make_async_remote_copy(
                    source.at[peer, channels], target.at[me, channels], send_sem.at[pair], recv_sem.at[pair, me],
                    device_id=(sec, peer), device_id_type=MESH,
                ).start()

            return carry

        def here(pair):
            def one(peer, carry):
                @pl.when(peer != me)
                def _():
                    landed = target.at[peer, pl.ds(pair * PAIR, PAIR)]
                    pltpu.make_async_copy(landed, landed, recv_sem.at[pair, peer]).wait()

                return carry

            lax.fori_loop(0, parts, one, 0)

        def left_here():
            for pair in range(pairs):
                others = source.at[pl.ds(0, parts - 1), pl.ds(0, PAIR)]
                pltpu.make_async_copy(others, others, send_sem.at[pair]).wait()

        return send, here, left_here

    send, product_here, product_left = over(prod, chan, to_send, to_recv)
    send_back, conv_here, conv_left = over(conv, ret, back_send, back_recv)

    def to_all(send_one, pair):
        for turn in turns:
            first = quarter(turn) * per_tile
            lax.fori_loop(
                0, per_tile,
                lambda offset, carry, first=first: send_one(pair, first + lax.rem(me + offset, per_tile), carry), 0,
            )

    ring_finish(0)
    ring_finish(1)
    lax.fori_loop(0, tiles, product_tile, 0)
    chan[me] = prod[me]

    def late_step():
        nonlocal late_done
        if late_done < steps:
            late_done += 1
            ring_step(late, late_done)

    late_step()
    for pair in range(1, pairs):
        to_all(send, pair)


    def convolve(pair):
        data = chan[:, pl.ds(pair * PAIR, PAIR), :].astype(F32)
        columns = jnp.concatenate(
            [data[:, :FEW].reshape(rows_k, block), data[:, FEW:].reshape(rows_k, block)], axis=1
        )
        outer_rows(pair, columns.astype(BF16), None)
        for group in (2 * pair, 2 * pair + 1):
            lanes = pl.ds(group * block, block)
            data = inner_rows(group)
            real, imag = data[:, :block], data[:, block:]
            filter_real, filter_imag = spec[group, :, pl.ds(0, block)], spec[group, :, pl.ds(block, block)]
            points = jnp.concatenate(
                [real * filter_real - imag * filter_imag, real * filter_imag + imag * filter_real], axis=1
            )
            high, low = split(points)
            value = dot3(high, low, di_hi[...], di_lo[...])
            real, imag = value[:, :block], value[:, block:]
            cos, sin = tw_cos[...], tw_sin[...]
            above, below = pl.ds(0, rows_k), pl.ds(rows_k, rows_k)
            back_hi[above, lanes], back_lo[above, lanes] = split(real * cos - imag * sin)
            back_hi[below, lanes], back_lo[below, lanes] = split(imag * cos + real * sin)
        lanes = pl.ds(2 * block * pair, 2 * block)
        value = dot3(gi_hi[...], gi_lo[...], back_hi[:, lanes], back_lo[:, lanes])
        whole = jnp.concatenate(
            [value[:, :block].reshape(parts, FEW, block), value[:, block:].reshape(parts, FEW, block)], axis=1
        )
        conv[:, pl.ds(pair * PAIR, PAIR), :] = whole.astype(BF16)

    for pair in range(pairs):
        product_here(pair)
        convolve(pair)
        to_all(send_back, pair)
        late_step()
    ret[me] = conv[me]
    while late_done < steps:
        late_step()

    def query_tile(index, carry):
        value = mixed(2, index * tile, 0).T
        query[pl.ds(pl.multiple_of(index * per_tile, per_tile), per_tile)] = value.reshape(per_tile, depth, tokens)
        return carry

    ring_finish(2)
    lax.fori_loop(0, tiles, query_tile, 0)
    ring_finish(3)

    for pair in range(pairs):
        conv_here(pair)
    gates = (query[...] * ret[...].astype(F32)).astype(BF16).reshape(width, tokens)
    for index in range(tiles):
        span = pl.ds(index * tile, tile)
        mixing = dot(w[3, span, :], gates)
        out[0, :, span] = (rows_in[:, span].astype(F32) + mixing.T).astype(BF16)

    relay.wait_send()
    relay_halo.wait_send()
    for stream in key_value + late:
        kind, first, count = streams[stream]
        all_sent = w.at[kind, pl.ds(0, (chips - 1) * depth), pl.ds(first, count)]
        pltpu.make_async_copy(all_sent, all_sent, ring_send.at[stream]).wait()
    for kind in range(4):
        all_sent = w.at[kind, pl.ds(0, chips * depth)]
        pltpu.make_async_copy(all_sent, all_sent, pair_send.at[kind]).wait()
    product_left()
    conv_left()


def shards(activations, norm_gain, in_weight, short_weight, long_filter, out_weight):
    sections, parts = lax.axis_size("section"), lax.axis_size("ctx")
    chips = parts // 2
    tokens, width = activations.shape[1:]
    depth = width // parts
    rows_k = parts * FEW
    groups, pairs = depth // FEW, depth // PAIR
    tables = [jnp.asarray(table) for table in transform_tables(parts, tokens)]
    in_hbm = pl.BlockSpec(memory_space=pltpu.HBM)
    in_vmem = pl.BlockSpec(memory_space=pltpu.VMEM)
    tile = min(256, width)
    scratch = [
        pltpu.VMEM((4, width, width), BF16),
        pltpu.VMEM((tokens, width), BF16),
        pltpu.VMEM((HALO, width), BF16),
        pltpu.VMEM((HALO + tokens, width), BF16),
        pltpu.VMEM((2, HALO + tokens, tile), F32),
        pltpu.VMEM((parts, depth, tokens), BF16),
        pltpu.VMEM((parts, depth, tokens), BF16),
        pltpu.VMEM((parts, depth, tokens), F32),
        pltpu.VMEM((2 * rows_k, groups * tokens), F32),
        pltpu.VMEM((groups, rows_k, 2 * tokens), F32),
        pltpu.VMEM((2 * rows_k, groups * tokens), BF16),
        pltpu.VMEM((2 * rows_k, groups * tokens), BF16),
        pltpu.VMEM((parts, depth, tokens), BF16),
        pltpu.VMEM((parts, depth, tokens), BF16),
        pltpu.VMEM(long_filter.shape[1:], F32),
        *[pltpu.VMEM(table.shape, F32) for table in tables],
        *[pltpu.VMEM(table.shape, BF16) for table in tables[:4] for _ in range(2)],
        pltpu.SemaphoreType.DMA((4,)),
        pltpu.SemaphoreType.DMA((4, parts)),
        pltpu.SemaphoreType.DMA((4,)),
        pltpu.SemaphoreType.DMA((4, chips)),
        pltpu.SemaphoreType.DMA((4,)),
        pltpu.SemaphoreType.DMA((2,)),
        pltpu.SemaphoreType.DMA((2,)),
        pltpu.SemaphoreType.DMA((pairs,)),
        pltpu.SemaphoreType.DMA((pairs, parts)),
        pltpu.SemaphoreType.DMA((pairs,)),
        pltpu.SemaphoreType.DMA((pairs, parts)),
        pltpu.SemaphoreType.DMA((len(tables) + 1,)),
    ]
    return pl.pallas_call(
        functools.partial(kernel, sections, chips, width, tokens),
        out_shape=pltpu.VMEM(activations.shape, BF16),
        in_specs=[in_hbm, in_vmem, in_hbm, in_vmem] + [in_hbm] * (2 + len(tables)),
        out_specs=in_vmem,
        scratch_shapes=scratch,
        compiler_params=pltpu.CompilerParams(
            collective_id=0, has_side_effects=True, vmem_limit_bytes=63 * 1024 * 1024
        ),
    )(
        activations, norm_gain, in_weight, jnp.transpose(short_weight, (1, 0, 2)), long_filter,
        jnp.swapaxes(out_weight, 1, 2), *tables,
    )


def solution(mesh):
    return jax.shard_map(
        shards,
        mesh=mesh,
        in_specs=(
            P("section", "ctx", None),
            P("section", None),
            P("section", "ctx", None),
            P("section", None, None),
            P("section", "ctx", None),
            P("section", None, "ctx"),
        ),
        out_specs=P("section", "ctx", None),
        check_vma=False,
    )
```

```python
import functools
import math

import jax
import jax.numpy as jnp
import numpy as np
from jax import lax
from jax.experimental import pallas as pl
from jax.experimental.pallas import tpu as pltpu
from jax.sharding import PartitionSpec as P

MESH = pl.DeviceIdType.MESH
F32, BF16 = jnp.float32, jnp.bfloat16
HALO = 16
FEW = 8
PAIR = 2 * FEW


def transform_tables(parts, block):
    points = parts * block
    k = np.arange(parts)[:, None] + 0.25
    outer = 2.0 * math.pi * k * np.arange(parts)[None, :] / parts
    eye = np.eye(FEW)
    forward = np.concatenate([np.kron(np.cos(outer), eye), np.kron(-np.sin(outer), eye)], axis=0)
    inner = 2.0 * math.pi * np.outer(np.arange(block), np.arange(block)) / block
    cos, sin = np.cos(inner), np.sin(inner)
    inner_forward = np.block([[cos, -sin], [sin, cos]])
    inner_inverse = np.block([[cos, sin], [-sin, cos]])
    twist = np.repeat(2.0 * math.pi * k * np.arange(block)[None, :] / points, FEW, axis=0)
    tables = (forward, forward.T, inner_forward, inner_inverse, np.cos(twist), np.sin(twist))
    return [np.asarray(table, np.float32) for table in tables]


def split(value):
    high = value.astype(BF16)
    return high, (value - high.astype(F32)).astype(BF16)


def dot(a, b):
    return jnp.dot(a, b, preferred_element_type=F32)


def dot3(a_high, a_low, b_high, b_low):
    return dot(a_high, b_high) + (dot(a_high, b_low) + dot(a_low, b_high))


def kernel(
    sections, chips, width, tokens,
    act, gain_in, in_w, taps_in, filt, out_w, g_in, gi_in, d_in, di_in, tw_cos_in, tw_sin_in,
    out,
    w, rows_in, halo_in, normed, feat, prod, chan, query, outer, spec, back_hi, back_lo, conv, ret,
    gain, taps, fil, g_all, gi_all, d_all, di_all, tw_cos, tw_sin, g_hi, g_lo, gi_hi, gi_lo, d_hi, d_lo, di_hi, di_lo,
    ring_send, ring_recv, pair_send, pair_recv, own_sem, relay_send, relay_recv, to_send, to_recv, back_send, back_recv,
    load_sem,
):
    parts = 2 * chips
    depth = width // parts
    block = tokens
    rows_k = parts * FEW
    pairs = depth // PAIR
    tile = min(256, width)
    sec, me = lax.axis_index("section"), lax.axis_index("ctx")
    core = lax.rem(me, 2)
    chip = lax.div(me, 2)

    def at(chip_index, core_index):
        return lax.rem(chip_index + 2 * chips, chips) * 2 + core_index

    right, left, sibling = at(chip + 1, core), at(chip - 1, core), at(chip, 1 - core)
    next_sec, prev_sec = lax.rem(sec + 1, sections), lax.rem(sec + sections - 1, sections)
    next_ctx, prev_ctx = lax.rem(me + 1, parts), lax.rem(me + parts - 1, parts)

    barrier = pltpu.get_barrier_semaphore()
    for peer in (left, right, sibling):
        pl.semaphore_signal(barrier, inc=1, device_id=(sec, peer), device_id_type=MESH)
    pl.semaphore_signal(barrier, inc=1, device_id=(prev_sec, me), device_id_type=MESH)
    pl.semaphore_signal(barrier, inc=1, device_id=(prev_sec, prev_ctx), device_id_type=MESH)
    pl.semaphore_wait(barrier, 5)

    relay = pltpu.make_async_remote_copy(
        act.at[0], rows_in, relay_send.at[0], relay_recv.at[0],
        device_id=(next_sec, me), device_id_type=MESH,
    )
    relay_halo = pltpu.make_async_remote_copy(
        act.at[0, pl.ds(tokens - HALO, HALO)], halo_in, relay_send.at[1], relay_recv.at[1],
        device_id=(next_sec, next_ctx), device_id_type=MESH,
    )

    hops = [(chips // 2, chips - 1 - chips // 2), (chips - 1 - chips // 2, chips // 2)]
    sources = [
        in_w.at[0, :, pl.ds(width, width)], in_w.at[0, :, pl.ds(2 * width, width)],
        in_w.at[0, :, pl.ds(0, width)], out_w.at[0],
    ]

    streams = [(0, 0, width), (1, 0, width), (2, 0, width), (3, 0, width)]
    key_value, late = (0, 1), (2, 3)

    def rows_of(owner):
        return pl.ds(pl.multiple_of(owner * depth, depth), depth)

    def ring_copy(stream, source, owner, target):
        kind, first, count = streams[stream]
        return pltpu.make_async_remote_copy(
            source, w.at[kind, rows_of(owner), pl.ds(first, count)],
            ring_send.at[stream], ring_recv.at[stream, owner],
            device_id=(sec, target), device_id_type=MESH,
        )

    def sibling_copy(kind, source, owner):
        return pltpu.make_async_remote_copy(
            source, w.at[kind, rows_of(owner)], pair_send.at[kind], pair_recv.at[kind, lax.div(owner, 2)],
            device_id=(sec, sibling), device_id_type=MESH,
        )

    def ring_start(group):
        for stream in group:
            kind, first, count = streams[stream]
            own = sources[kind].at[:, pl.ds(first, count)]
            for count, target in zip(hops[stream % 2], (right, left)):
                if count:
                    ring_copy(stream, own, me, target).start()
        for kind in sorted({streams[stream][0] for stream in group}):
            sibling_copy(kind, sources[kind], me).start()
            pltpu.make_async_copy(sources[kind], w.at[kind, rows_of(me)], own_sem.at[kind]).start()

    def ring_step(group, step):
        for stream in group:
            kind, first, count = streams[stream]
            ways = ((at(chip - step, core), right), (at(chip + step, core), left))
            for far, (owner, target) in zip(hops[stream % 2], ways):
                if step > far:
                    continue
                here = w.at[kind, rows_of(owner), pl.ds(first, count)]
                pltpu.make_async_copy(here, here, ring_recv.at[stream, owner]).wait()
                if step < far:
                    ring_copy(stream, here, owner, target).start()
                if first + count == width:
                    sibling_copy(kind, w.at[kind, rows_of(owner)], owner).start()

    def ring_finish(kind):
        pltpu.make_async_copy(sources[kind], w.at[kind, rows_of(me)], own_sem.at[kind]).wait()

        def other(index, carry):
            here = w.at[kind, rows_of(2 * index + 1 - core)]
            pltpu.make_async_copy(here, here, pair_recv.at[kind, index]).wait()
            return carry

        lax.fori_loop(0, chips, other, 0)

    ring_start(key_value)
    relay.start()
    relay_halo.start()
    ring_start(late)

    loads = [
        pltpu.make_async_copy(source, target, load_sem.at[slot])
        for slot, (source, target) in enumerate(
            [
                (filt.at[0], fil), (g_in, g_all), (d_in, d_all), (tw_cos_in, tw_cos), (tw_sin_in, tw_sin),
                (di_in, di_all), (gi_in, gi_all), (gain_in, gain), (taps_in, taps),
            ]
        )
    ]
    for load in loads:
        load.start()

    def outer_rows(pair, columns_high, columns_low):
        lanes = pl.ds(2 * block * pair, 2 * block)
        for index in range(2):
            rows = pl.ds(index * rows_k, rows_k)
            value = dot(g_hi[rows, :], columns_high) + dot(g_lo[rows, :], columns_high)
            if columns_low is not None:
                value = value + dot(g_hi[rows, :], columns_low)
            outer[rows, lanes] = value

    def inner_rows(group):
        lanes = pl.ds(group * block, block)
        real, imag = outer[pl.ds(0, rows_k), lanes], outer[pl.ds(rows_k, rows_k), lanes]
        cos, sin = tw_cos[...], tw_sin[...]
        turned = jnp.concatenate([real * cos + imag * sin, imag * cos - real * sin], axis=1)
        high, low = split(turned)
        return dot3(high, low, d_hi[...], d_lo[...])

    def filter_outer(pair):
        columns = [
            jnp.concatenate(
                [fil[pl.ds(group * FEW, FEW), pl.ds(n * block, block)] for n in range(parts)], axis=0
            )
            for group in (2 * pair, 2 * pair + 1)
        ]
        high, low = split(jnp.concatenate(columns, axis=1))
        outer_rows(pair, high, low)

    def filter_inner(group):
        spec[group] = inner_rows(group) * (1.0 / (parts * block))

    def norm(values, gain_row):
        values = values.astype(F32)
        scale = lax.rsqrt(jnp.mean(values * values, axis=-1, keepdims=True) + 1e-06)
        return values * scale * gain_row

    def norm_rows():
        wait_loads(7, 2)
        relay.wait_recv()
        relay_halo.wait_recv()
        before = norm(halo_in[...], gain[...])
        normed[pl.ds(0, HALO), :] = jnp.where(me > 0, before, jnp.zeros_like(before)).astype(BF16)
        normed[pl.ds(HALO, tokens), :] = norm(rows_in[...], gain[...]).astype(BF16)

    def wait_loads(first, count):
        for load in loads[first : first + count]:
            load.wait()

    steps = chips // 2
    def split_table(whole, high, low):
        high[...], low[...] = split(whole[...])

    between = [
        lambda: (wait_loads(0, 2), split_table(g_all, g_hi, g_lo)),
        lambda: [filter_outer(pair) for pair in range(pairs)],
        lambda: (wait_loads(2, 3), split_table(d_all, d_hi, d_lo), filter_inner(0), filter_inner(1)),
        lambda: [filter_inner(group) for group in range(2, 2 * pairs)],
        norm_rows,
        lambda: (wait_loads(5, 2), split_table(di_all, di_hi, di_lo), split_table(gi_all, gi_hi, gi_lo)),
    ]
    late_done = 0
    for step in range(1, steps + 1):
        ring_step(key_value, step)
        if between:
            between.pop(0)()
        if 2 <= step < steps:
            late_done += 1
            ring_step(late, late_done)
    for piece in between:
        piece()
    def mixed(kind, column, place):
        columns = pl.ds(pl.multiple_of(column, tile), tile)
        feat[place] = dot(normed[...], w[kind, :, columns])
        base = (0 if kind == 2 else width * (kind + 1)) + column
        weights = [taps[i, :, pl.ds(pl.multiple_of(base, tile), tile)] for i in range(3)]
        value = weights[0] * feat[place, pl.ds(HALO, tokens), :]
        value = value + weights[1] * feat[place, pl.ds(HALO - 1, tokens), :]
        return value + weights[2] * feat[place, pl.ds(HALO - 2, tokens), :]

    tiles = width // tile
    per_tile = tile // depth

    turns = [2, 1, 3, 0] if tiles == 4 else [*range(1, tiles), 0]

    def quarter(turn):
        return lax.rem(lax.div(me, per_tile) + turn, tiles)

    def product_tile(index, carry):
        at_tile = lax.rem(lax.div(me, per_tile) + 2 + index, tiles)
        column = at_tile * tile
        value = (mixed(0, column, 0) * mixed(1, column, 1)).T.astype(BF16)
        first = pl.multiple_of(at_tile * per_tile, per_tile)
        prod[pl.ds(first, per_tile)] = value.reshape(per_tile, depth, tokens)

        lax.fori_loop(0, per_tile, lambda offset, inner: send(0, first + offset, inner), 0)
        return carry

    def over(source, target, send_sem, recv_sem):
        def send(pair, peer, carry):
            channels = pl.ds(pair * PAIR, PAIR)

            @pl.when(peer != me)
            def _():
                pltpu.make_async_remote_copy(
                    source.at[peer, channels], target.at[me, channels], send_sem.at[pair], recv_sem.at[pair, me],
                    device_id=(sec, peer), device_id_type=MESH,
                ).start()

            return carry

        def here(pair):
            def one(peer, carry):
                @pl.when(peer != me)
                def _():
                    landed = target.at[peer, pl.ds(pair * PAIR, PAIR)]
                    pltpu.make_async_copy(landed, landed, recv_sem.at[pair, peer]).wait()

                return carry

            lax.fori_loop(0, parts, one, 0)

        def left_here():
            for pair in range(pairs):
                others = source.at[pl.ds(0, parts - 1), pl.ds(0, PAIR)]
                pltpu.make_async_copy(others, others, send_sem.at[pair]).wait()

        return send, here, left_here

    send, product_here, product_left = over(prod, chan, to_send, to_recv)
    send_back, conv_here, conv_left = over(conv, ret, back_send, back_recv)

    def to_all(send_one, pair):
        for turn in turns:
            first = quarter(turn) * per_tile
            lax.fori_loop(
                0, per_tile,
                lambda offset, carry, first=first: send_one(pair, first + lax.rem(me + offset, per_tile), carry), 0,
            )

    ring_finish(0)
    ring_finish(1)
    lax.fori_loop(0, tiles, product_tile, 0)
    chan[me] = prod[me]

    def late_step():
        nonlocal late_done
        if late_done < steps:
            late_done += 1
            ring_step(late, late_done)

    late_step()
    for pair in range(1, pairs):
        to_all(send, pair)


    def convolve(pair):
        data = chan[:, pl.ds(pair * PAIR, PAIR), :].astype(F32)
        columns = jnp.concatenate(
            [data[:, :FEW].reshape(rows_k, block), data[:, FEW:].reshape(rows_k, block)], axis=1
        )
        outer_rows(pair, columns.astype(BF16), None)
        for group in (2 * pair, 2 * pair + 1):
            lanes = pl.ds(group * block, block)
            data = inner_rows(group)
            real, imag = data[:, :block], data[:, block:]
            filter_real, filter_imag = spec[group, :, pl.ds(0, block)], spec[group, :, pl.ds(block, block)]
            points = jnp.concatenate(
                [real * filter_real - imag * filter_imag, real * filter_imag + imag * filter_real], axis=1
            )
            high, low = split(points)
            value = dot3(high, low, di_hi[...], di_lo[...])
            real, imag = value[:, :block], value[:, block:]
            cos, sin = tw_cos[...], tw_sin[...]
            above, below = pl.ds(0, rows_k), pl.ds(rows_k, rows_k)
            back_hi[above, lanes], back_lo[above, lanes] = split(real * cos - imag * sin)
            back_hi[below, lanes], back_lo[below, lanes] = split(imag * cos + real * sin)
        lanes = pl.ds(2 * block * pair, 2 * block)
        value = dot3(gi_hi[...], gi_lo[...], back_hi[:, lanes], back_lo[:, lanes])
        whole = jnp.concatenate(
            [value[:, :block].reshape(parts, FEW, block), value[:, block:].reshape(parts, FEW, block)], axis=1
        )
        conv[:, pl.ds(pair * PAIR, PAIR), :] = whole.astype(BF16)

    for pair in range(pairs):
        product_here(pair)
        convolve(pair)
        to_all(send_back, pair)
        late_step()
    ret[me] = conv[me]
    while late_done < steps:
        late_step()

    def query_tile(index, carry):
        value = mixed(2, index * tile, 0).T
        query[pl.ds(pl.multiple_of(index * per_tile, per_tile), per_tile)] = value.reshape(per_tile, depth, tokens)
        return carry

    ring_finish(2)
    lax.fori_loop(0, tiles, query_tile, 0)
    ring_finish(3)

    for pair in range(pairs):
        conv_here(pair)
    gates = (query[...] * ret[...].astype(F32)).astype(BF16).reshape(width, tokens)
    for index in range(tiles):
        span = pl.ds(index * tile, tile)
        mixing = dot(w[3, span, :], gates)
        out[0, :, span] = (rows_in[:, span].astype(F32) + mixing.T).astype(BF16)

    relay.wait_send()
    relay_halo.wait_send()
    for stream in key_value + late:
        kind, first, count = streams[stream]
        all_sent = w.at[kind, pl.ds(0, (chips - 1) * depth), pl.ds(first, count)]
        pltpu.make_async_copy(all_sent, all_sent, ring_send.at[stream]).wait()
    for kind in range(4):
        all_sent = w.at[kind, pl.ds(0, chips * depth)]
        pltpu.make_async_copy(all_sent, all_sent, pair_send.at[kind]).wait()
    product_left()
    conv_left()


def shards(activations, norm_gain, in_weight, short_weight, long_filter, out_weight):
    sections, parts = lax.axis_size("section"), lax.axis_size("ctx")
    chips = parts // 2
    tokens, width = activations.shape[1:]
    depth = width // parts
    rows_k = parts * FEW
    groups, pairs = depth // FEW, depth // PAIR
    tables = [jnp.asarray(table) for table in transform_tables(parts, tokens)]
    in_hbm = pl.BlockSpec(memory_space=pltpu.HBM)
    in_vmem = pl.BlockSpec(memory_space=pltpu.VMEM)
    tile = min(256, width)
    scratch = [
        pltpu.VMEM((4, width, width), BF16),
        pltpu.VMEM((tokens, width), BF16),
        pltpu.VMEM((HALO, width), BF16),
        pltpu.VMEM((HALO + tokens, width), BF16),
        pltpu.VMEM((2, HALO + tokens, tile), F32),
        pltpu.VMEM((parts, depth, tokens), BF16),
        pltpu.VMEM((parts, depth, tokens), BF16),
        pltpu.VMEM((parts, depth, tokens), F32),
        pltpu.VMEM((2 * rows_k, groups * tokens), F32),
        pltpu.VMEM((groups, rows_k, 2 * tokens), F32),
        pltpu.VMEM((2 * rows_k, groups * tokens), BF16),
        pltpu.VMEM((2 * rows_k, groups * tokens), BF16),
        pltpu.VMEM((parts, depth, tokens), BF16),
        pltpu.VMEM((parts, depth, tokens), BF16),
        pltpu.VMEM(norm_gain.shape, F32),
        pltpu.VMEM((3, 1, 3 * width), F32),
        pltpu.VMEM(long_filter.shape[1:], F32),
        *[pltpu.VMEM(table.shape, F32) for table in tables],
        *[pltpu.VMEM(table.shape, BF16) for table in tables[:4] for _ in range(2)],
        pltpu.SemaphoreType.DMA((4,)),
        pltpu.SemaphoreType.DMA((4, parts)),
        pltpu.SemaphoreType.DMA((4,)),
        pltpu.SemaphoreType.DMA((4, chips)),
        pltpu.SemaphoreType.DMA((4,)),
        pltpu.SemaphoreType.DMA((2,)),
        pltpu.SemaphoreType.DMA((2,)),
        pltpu.SemaphoreType.DMA((pairs,)),
        pltpu.SemaphoreType.DMA((pairs, parts)),
        pltpu.SemaphoreType.DMA((pairs,)),
        pltpu.SemaphoreType.DMA((pairs, parts)),
        pltpu.SemaphoreType.DMA((len(tables) + 3,)),
    ]
    return pl.pallas_call(
        functools.partial(kernel, sections, chips, width, tokens),
        out_shape=pltpu.VMEM(activations.shape, BF16),
        in_specs=[in_hbm] * (6 + len(tables)),
        out_specs=in_vmem,
        scratch_shapes=scratch,
        compiler_params=pltpu.CompilerParams(
            collective_id=0, has_side_effects=True, vmem_limit_bytes=63 * 1024 * 1024
        ),
    )(
        activations, norm_gain, in_weight, jnp.transpose(short_weight, (1, 0, 2)), long_filter,
        jnp.swapaxes(out_weight, 1, 2), *tables,
    )


def solution(mesh):
    return jax.shard_map(
        shards,
        mesh=mesh,
        in_specs=(
            P("section", "ctx", None),
            P("section", None),
            P("section", "ctx", None),
            P("section", None, None),
            P("section", "ctx", None),
            P("section", None, "ctx"),
        ),
        out_specs=P("section", "ctx", None),
        check_vma=False,
    )
```

```python
import functools
import math

import jax
import jax.numpy as jnp
import numpy as np
from jax import lax
from jax.experimental import pallas as pl
from jax.experimental.pallas import tpu as pltpu
from jax.sharding import PartitionSpec as P

MESH = pl.DeviceIdType.MESH
F32, BF16 = jnp.float32, jnp.bfloat16
HALO = 16
FEW = 8
PAIR = 2 * FEW


def transform_tables(parts, block):
    points = parts * block
    k = np.arange(parts)[:, None] + 0.25
    outer = 2.0 * math.pi * k * np.arange(parts)[None, :] / parts
    eye = np.eye(FEW)
    forward = np.concatenate([np.kron(np.cos(outer), eye), np.kron(-np.sin(outer), eye)], axis=0)
    inner = 2.0 * math.pi * np.outer(np.arange(block), np.arange(block)) / block
    cos, sin = np.cos(inner), np.sin(inner)
    inner_forward = np.block([[cos, -sin], [sin, cos]])
    inner_inverse = np.block([[cos, sin], [-sin, cos]])
    twist = np.repeat(2.0 * math.pi * k * np.arange(block)[None, :] / points, FEW, axis=0)
    tables = (forward, forward.T, inner_forward, inner_inverse, np.cos(twist), np.sin(twist))
    return [np.asarray(table, np.float32) for table in tables]


def split(value):
    high = value.astype(BF16)
    return high, (value - high.astype(F32)).astype(BF16)


def dot(a, b):
    return jnp.dot(a, b, preferred_element_type=F32)


def dot3(a_high, a_low, b_high, b_low):
    return dot(a_high, b_high) + (dot(a_high, b_low) + dot(a_low, b_high))


def kernel(
    sections, chips, width, tokens,
    act, gain_in, in_w, taps_in, filt, out_w, g_in, gi_in, d_in, di_in, tw_cos_in, tw_sin_in,
    out,
    w, rows_in, halo_in, normed, feat, prod, chan, query, outer, spec, back_hi, back_lo, conv, ret,
    gain, taps, fil, g_all, gi_all, d_all, di_all, tw_cos, tw_sin, g_hi, g_lo, gi_hi, gi_lo, d_hi, d_lo, di_hi, di_lo,
    ring_send, ring_recv, pair_send, pair_recv, own_sem, relay_send, relay_recv, to_send, to_recv, back_send, back_recv,
    load_sem,
):
    parts = 2 * chips
    depth = width // parts
    block = tokens
    rows_k = parts * FEW
    pairs = depth // PAIR
    tile = min(256, width)
    sec, me = lax.axis_index("section"), lax.axis_index("ctx")
    core = lax.rem(me, 2)
    chip = lax.div(me, 2)

    def at(chip_index, core_index):
        return lax.rem(chip_index + 2 * chips, chips) * 2 + core_index

    right, left, sibling = at(chip + 1, core), at(chip - 1, core), at(chip, 1 - core)
    next_sec, prev_sec = lax.rem(sec + 1, sections), lax.rem(sec + sections - 1, sections)
    next_ctx, prev_ctx = lax.rem(me + 1, parts), lax.rem(me + parts - 1, parts)

    barrier = pltpu.get_barrier_semaphore()
    for peer in (left, right, sibling):
        pl.semaphore_signal(barrier, inc=1, device_id=(sec, peer), device_id_type=MESH)
    pl.semaphore_signal(barrier, inc=1, device_id=(prev_sec, me), device_id_type=MESH)
    pl.semaphore_signal(barrier, inc=1, device_id=(prev_sec, prev_ctx), device_id_type=MESH)
    pl.semaphore_wait(barrier, 5)

    relay = pltpu.make_async_remote_copy(
        act.at[0], rows_in, relay_send.at[0], relay_recv.at[0],
        device_id=(next_sec, me), device_id_type=MESH,
    )
    relay_halo = pltpu.make_async_remote_copy(
        act.at[0, pl.ds(tokens - HALO, HALO)], halo_in, relay_send.at[1], relay_recv.at[1],
        device_id=(next_sec, next_ctx), device_id_type=MESH,
    )

    hops = [(chips // 2, chips - 1 - chips // 2), (chips - 1 - chips // 2, chips // 2)]
    sources = [
        in_w.at[0, :, pl.ds(width, width)], in_w.at[0, :, pl.ds(2 * width, width)],
        in_w.at[0, :, pl.ds(0, width)], out_w.at[0],
    ]

    streams = [(0, 0, width), (1, 0, width), (2, 0, width), (3, 0, width)]
    key_value, late = (0, 1), (2, 3)

    def rows_of(owner):
        return pl.ds(pl.multiple_of(owner * depth, depth), depth)

    def ring_copy(stream, source, owner, target):
        kind, first, count = streams[stream]
        return pltpu.make_async_remote_copy(
            source, w.at[kind, rows_of(owner), pl.ds(first, count)],
            ring_send.at[stream], ring_recv.at[stream, owner],
            device_id=(sec, target), device_id_type=MESH,
        )

    def sibling_copy(kind, source, owner):
        return pltpu.make_async_remote_copy(
            source, w.at[kind, rows_of(owner)], pair_send.at[kind], pair_recv.at[kind],
            device_id=(sec, sibling), device_id_type=MESH,
        )

    def ring_start(group):
        for stream in group:
            kind, first, count = streams[stream]
            own = sources[kind].at[:, pl.ds(first, count)]
            for count, target in zip(hops[stream % 2], (right, left)):
                if count:
                    ring_copy(stream, own, me, target).start()
        for kind in sorted({streams[stream][0] for stream in group}):
            sibling_copy(kind, sources[kind], me).start()
            pltpu.make_async_copy(sources[kind], w.at[kind, rows_of(me)], own_sem.at[kind]).start()

    def ring_step(group, step):
        for stream in group:
            kind, first, count = streams[stream]
            ways = ((at(chip - step, core), right), (at(chip + step, core), left))
            for far, (owner, target) in zip(hops[stream % 2], ways):
                if step > far:
                    continue
                here = w.at[kind, rows_of(owner), pl.ds(first, count)]
                pltpu.make_async_copy(here, here, ring_recv.at[stream, owner]).wait()
                if step < far:
                    ring_copy(stream, here, owner, target).start()
                if first + count == width:
                    sibling_copy(kind, w.at[kind, rows_of(owner)], owner).start()

    def ring_finish(kind):
        pltpu.make_async_copy(sources[kind], w.at[kind, rows_of(me)], own_sem.at[kind]).wait()

        landed = w.at[kind, pl.ds(0, chips * depth)]
        pltpu.make_async_copy(landed, landed, pair_recv.at[kind]).wait()

    ring_start(key_value)
    relay.start()
    relay_halo.start()
    ring_start(late)

    loads = [
        pltpu.make_async_copy(source, target, load_sem.at[slot])
        for slot, (source, target) in enumerate(
            [
                (filt.at[0], fil), (g_in, g_all), (d_in, d_all), (tw_cos_in, tw_cos), (tw_sin_in, tw_sin),
                (di_in, di_all), (gi_in, gi_all), (gain_in, gain), (taps_in, taps),
            ]
        )
    ]
    for load in loads:
        load.start()

    def outer_rows(pair, columns_high, columns_low):
        lanes = pl.ds(2 * block * pair, 2 * block)
        for index in range(2):
            rows = pl.ds(index * rows_k, rows_k)
            value = dot(g_hi[rows, :], columns_high) + dot(g_lo[rows, :], columns_high)
            if columns_low is not None:
                value = value + dot(g_hi[rows, :], columns_low)
            outer[rows, lanes] = value

    def inner_rows(group):
        lanes = pl.ds(group * block, block)
        real, imag = outer[pl.ds(0, rows_k), lanes], outer[pl.ds(rows_k, rows_k), lanes]
        cos, sin = tw_cos[...], tw_sin[...]
        turned = jnp.concatenate([real * cos + imag * sin, imag * cos - real * sin], axis=1)
        high, low = split(turned)
        return dot3(high, low, d_hi[...], d_lo[...])

    def filter_outer(pair):
        columns = [
            jnp.concatenate(
                [fil[pl.ds(group * FEW, FEW), pl.ds(n * block, block)] for n in range(parts)], axis=0
            )
            for group in (2 * pair, 2 * pair + 1)
        ]
        high, low = split(jnp.concatenate(columns, axis=1))
        outer_rows(pair, high, low)

    def filter_inner(group):
        spec[group] = inner_rows(group) * (1.0 / (parts * block))

    def norm(values, gain_row):
        values = values.astype(F32)
        scale = lax.rsqrt(jnp.mean(values * values, axis=-1, keepdims=True) + 1e-06)
        return values * scale * gain_row

    def norm_rows():
        wait_loads(7, 2)
        relay.wait_recv()
        relay_halo.wait_recv()
        before = norm(halo_in[...], gain[...])
        normed[pl.ds(0, HALO), :] = jnp.where(me > 0, before, jnp.zeros_like(before)).astype(BF16)
        normed[pl.ds(HALO, tokens), :] = norm(rows_in[...], gain[...]).astype(BF16)

    def wait_loads(first, count):
        for load in loads[first : first + count]:
            load.wait()

    steps = chips // 2
    def split_table(whole, high, low):
        high[...], low[...] = split(whole[...])

    between = [
        lambda: (wait_loads(0, 2), split_table(g_all, g_hi, g_lo)),
        lambda: [filter_outer(pair) for pair in range(pairs)],
        lambda: (wait_loads(2, 3), split_table(d_all, d_hi, d_lo), filter_inner(0), filter_inner(1)),
        lambda: [filter_inner(group) for group in range(2, 2 * pairs)],
        norm_rows,
        lambda: (wait_loads(5, 2), split_table(di_all, di_hi, di_lo), split_table(gi_all, gi_hi, gi_lo)),
    ]
    late_done = 0
    for step in range(1, steps + 1):
        ring_step(key_value, step)
        if between:
            between.pop(0)()
        if 2 <= step < steps:
            late_done += 1
            ring_step(late, late_done)
    for piece in between:
        piece()
    def mixed(kind, column, place):
        columns = pl.ds(pl.multiple_of(column, tile), tile)
        feat[place] = dot(normed[...], w[kind, :, columns])
        base = (0 if kind == 2 else width * (kind + 1)) + column
        weights = [taps[i, :, pl.ds(pl.multiple_of(base, tile), tile)] for i in range(3)]
        value = weights[0] * feat[place, pl.ds(HALO, tokens), :]
        value = value + weights[1] * feat[place, pl.ds(HALO - 1, tokens), :]
        return value + weights[2] * feat[place, pl.ds(HALO - 2, tokens), :]

    tiles = width // tile
    per_tile = tile // depth

    turns = [2, 1, 3, 0] if tiles == 4 else [*range(1, tiles), 0]

    def quarter(turn):
        return lax.rem(lax.div(me, per_tile) + turn, tiles)

    def product_tile(index, carry):
        at_tile = lax.rem(lax.div(me, per_tile) + 2 + index, tiles)
        column = at_tile * tile
        value = (mixed(0, column, 0) * mixed(1, column, 1)).T.astype(BF16)
        first = pl.multiple_of(at_tile * per_tile, per_tile)
        prod[pl.ds(first, per_tile)] = value.reshape(per_tile, depth, tokens)

        lax.fori_loop(0, per_tile, lambda offset, inner: send(0, first + offset, inner), 0)
        return carry

    def over(source, target, send_sem, recv_sem):
        def send(pair, peer, carry):
            channels = pl.ds(pair * PAIR, PAIR)

            @pl.when(peer != me)
            def _():
                pltpu.make_async_remote_copy(
                    source.at[peer, channels], target.at[me, channels], send_sem.at[pair], recv_sem.at[pair],
                    device_id=(sec, peer), device_id_type=MESH,
                ).start()

            return carry

        def here(pair):
            landed = target.at[pl.ds(0, parts - 1), pl.ds(0, PAIR)]
            pltpu.make_async_copy(landed, landed, recv_sem.at[pair]).wait()

        def left_here():
            for pair in range(pairs):
                others = source.at[pl.ds(0, parts - 1), pl.ds(0, PAIR)]
                pltpu.make_async_copy(others, others, send_sem.at[pair]).wait()

        return send, here, left_here

    send, product_here, product_left = over(prod, chan, to_send, to_recv)
    send_back, conv_here, conv_left = over(conv, ret, back_send, back_recv)

    def to_all(send_one, pair):
        for turn in turns:
            first = quarter(turn) * per_tile
            lax.fori_loop(
                0, per_tile,
                lambda offset, carry, first=first: send_one(pair, first + lax.rem(me + offset, per_tile), carry), 0,
            )

    ring_finish(0)
    ring_finish(1)
    lax.fori_loop(0, tiles, product_tile, 0)
    chan[me] = prod[me]

    def late_step():
        nonlocal late_done
        if late_done < steps:
            late_done += 1
            ring_step(late, late_done)

    late_step()
    for pair in range(1, pairs):
        to_all(send, pair)


    def convolve(pair):
        data = chan[:, pl.ds(pair * PAIR, PAIR), :].astype(F32)
        columns = jnp.concatenate(
            [data[:, :FEW].reshape(rows_k, block), data[:, FEW:].reshape(rows_k, block)], axis=1
        )
        outer_rows(pair, columns.astype(BF16), None)
        for group in (2 * pair, 2 * pair + 1):
            lanes = pl.ds(group * block, block)
            data = inner_rows(group)
            real, imag = data[:, :block], data[:, block:]
            filter_real, filter_imag = spec[group, :, pl.ds(0, block)], spec[group, :, pl.ds(block, block)]
            points = jnp.concatenate(
                [real * filter_real - imag * filter_imag, real * filter_imag + imag * filter_real], axis=1
            )
            high, low = split(points)
            value = dot3(high, low, di_hi[...], di_lo[...])
            real, imag = value[:, :block], value[:, block:]
            cos, sin = tw_cos[...], tw_sin[...]
            above, below = pl.ds(0, rows_k), pl.ds(rows_k, rows_k)
            back_hi[above, lanes], back_lo[above, lanes] = split(real * cos - imag * sin)
            back_hi[below, lanes], back_lo[below, lanes] = split(imag * cos + real * sin)
        lanes = pl.ds(2 * block * pair, 2 * block)
        value = dot3(gi_hi[...], gi_lo[...], back_hi[:, lanes], back_lo[:, lanes])
        whole = jnp.concatenate(
            [value[:, :block].reshape(parts, FEW, block), value[:, block:].reshape(parts, FEW, block)], axis=1
        )
        conv[:, pl.ds(pair * PAIR, PAIR), :] = whole.astype(BF16)

    for pair in range(pairs):
        product_here(pair)
        convolve(pair)
        to_all(send_back, pair)
        late_step()
    ret[me] = conv[me]
    while late_done < steps:
        late_step()

    def query_tile(index, carry):
        value = mixed(2, index * tile, 0).T
        query[pl.ds(pl.multiple_of(index * per_tile, per_tile), per_tile)] = value.reshape(per_tile, depth, tokens)
        return carry

    ring_finish(2)
    lax.fori_loop(0, tiles, query_tile, 0)
    ring_finish(3)

    for pair in range(pairs):
        conv_here(pair)
    gates = (query[...] * ret[...].astype(F32)).astype(BF16).reshape(width, tokens)
    for index in range(tiles):
        span = pl.ds(index * tile, tile)
        mixing = dot(w[3, span, :], gates)
        out[0, :, span] = (rows_in[:, span].astype(F32) + mixing.T).astype(BF16)

    relay.wait_send()
    relay_halo.wait_send()
    for stream in key_value + late:
        kind, first, count = streams[stream]
        all_sent = w.at[kind, pl.ds(0, (chips - 1) * depth), pl.ds(first, count)]
        pltpu.make_async_copy(all_sent, all_sent, ring_send.at[stream]).wait()
    for kind in range(4):
        all_sent = w.at[kind, pl.ds(0, chips * depth)]
        pltpu.make_async_copy(all_sent, all_sent, pair_send.at[kind]).wait()
    product_left()
    conv_left()


def shards(activations, norm_gain, in_weight, short_weight, long_filter, out_weight):
    sections, parts = lax.axis_size("section"), lax.axis_size("ctx")
    chips = parts // 2
    tokens, width = activations.shape[1:]
    depth = width // parts
    rows_k = parts * FEW
    groups, pairs = depth // FEW, depth // PAIR
    tables = [jnp.asarray(table) for table in transform_tables(parts, tokens)]
    in_hbm = pl.BlockSpec(memory_space=pltpu.HBM)
    in_vmem = pl.BlockSpec(memory_space=pltpu.VMEM)
    tile = min(256, width)
    scratch = [
        pltpu.VMEM((4, width, width), BF16),
        pltpu.VMEM((tokens, width), BF16),
        pltpu.VMEM((HALO, width), BF16),
        pltpu.VMEM((HALO + tokens, width), BF16),
        pltpu.VMEM((2, HALO + tokens, tile), F32),
        pltpu.VMEM((parts, depth, tokens), BF16),
        pltpu.VMEM((parts, depth, tokens), BF16),
        pltpu.VMEM((parts, depth, tokens), F32),
        pltpu.VMEM((2 * rows_k, groups * tokens), F32),
        pltpu.VMEM((groups, rows_k, 2 * tokens), F32),
        pltpu.VMEM((2 * rows_k, groups * tokens), BF16),
        pltpu.VMEM((2 * rows_k, groups * tokens), BF16),
        pltpu.VMEM((parts, depth, tokens), BF16),
        pltpu.VMEM((parts, depth, tokens), BF16),
        pltpu.VMEM(norm_gain.shape, F32),
        pltpu.VMEM((3, 1, 3 * width), F32),
        pltpu.VMEM(long_filter.shape[1:], F32),
        *[pltpu.VMEM(table.shape, F32) for table in tables],
        *[pltpu.VMEM(table.shape, BF16) for table in tables[:4] for _ in range(2)],
        pltpu.SemaphoreType.DMA((4,)),
        pltpu.SemaphoreType.DMA((4, parts)),
        pltpu.SemaphoreType.DMA((4,)),
        pltpu.SemaphoreType.DMA((4,)),
        pltpu.SemaphoreType.DMA((4,)),
        pltpu.SemaphoreType.DMA((2,)),
        pltpu.SemaphoreType.DMA((2,)),
        pltpu.SemaphoreType.DMA((pairs,)),
        pltpu.SemaphoreType.DMA((pairs,)),
        pltpu.SemaphoreType.DMA((pairs,)),
        pltpu.SemaphoreType.DMA((pairs,)),
        pltpu.SemaphoreType.DMA((len(tables) + 3,)),
    ]
    return pl.pallas_call(
        functools.partial(kernel, sections, chips, width, tokens),
        out_shape=pltpu.VMEM(activations.shape, BF16),
        in_specs=[in_hbm] * (6 + len(tables)),
        out_specs=in_vmem,
        scratch_shapes=scratch,
        compiler_params=pltpu.CompilerParams(
            collective_id=0, has_side_effects=True, vmem_limit_bytes=63 * 1024 * 1024
        ),
    )(
        activations, norm_gain, in_weight, jnp.transpose(short_weight, (1, 0, 2)), long_filter,
        jnp.swapaxes(out_weight, 1, 2), *tables,
    )


def solution(mesh):
    return jax.shard_map(
        shards,
        mesh=mesh,
        in_specs=(
            P("section", "ctx", None),
            P("section", None),
            P("section", "ctx", None),
            P("section", None, None),
            P("section", "ctx", None),
            P("section", None, "ctx"),
        ),
        out_specs=P("section", "ctx", None),
        check_vma=False,
    )
```

```python
import functools
import math

import jax
import jax.numpy as jnp
import numpy as np
from jax import lax
from jax.experimental import pallas as pl
from jax.experimental.pallas import tpu as pltpu
from jax.sharding import PartitionSpec as P

MESH = pl.DeviceIdType.MESH
F32, BF16 = jnp.float32, jnp.bfloat16
HALO = 16
FEW = 8
PAIR = 2 * FEW


def transform_tables(parts, block):
    points = parts * block
    k = np.arange(parts)[:, None] + 0.25
    outer = 2.0 * math.pi * k * np.arange(parts)[None, :] / parts
    eye = np.eye(FEW)
    forward = np.concatenate([np.kron(np.cos(outer), eye), np.kron(-np.sin(outer), eye)], axis=0)
    inner = 2.0 * math.pi * np.outer(np.arange(block), np.arange(block)) / block
    cos, sin = np.cos(inner), np.sin(inner)
    inner_forward = np.block([[cos, -sin], [sin, cos]])
    inner_inverse = np.block([[cos, sin], [-sin, cos]])
    twist = np.repeat(2.0 * math.pi * k * np.arange(block)[None, :] / points, FEW, axis=0)
    tables = (forward, forward.T, inner_forward, inner_inverse, np.cos(twist), np.sin(twist))
    return [np.asarray(table, np.float32) for table in tables]


def split(value):
    high = value.astype(BF16)
    return high, (value - high.astype(F32)).astype(BF16)


def dot(a, b):
    return jnp.dot(a, b, preferred_element_type=F32)


def dot3(a_high, a_low, b_high, b_low):
    return dot(a_high, b_high) + (dot(a_high, b_low) + dot(a_low, b_high))


def kernel(
    sections, chips, width, tokens,
    act, gain_in, in_w, taps_in, filt, out_w, g_in, gi_in, d_in, di_in, tw_cos_in, tw_sin_in,
    out,
    w, rows_in, halo_in, normed, feat, prod, chan, query, outer, spec, back_hi, back_lo, conv, ret,
    gain, taps, fil, g_all, gi_all, d_all, di_all, tw_cos, tw_sin, g_hi, g_lo, gi_hi, gi_lo, d_hi, d_lo, di_hi, di_lo,
    ring_send, ring_recv, pair_send, pair_recv, own_sem, relay_send, relay_recv, to_send, to_recv, back_send, back_recv,
    load_sem,
):
    parts = 2 * chips
    depth = width // parts
    block = tokens
    rows_k = parts * FEW
    pairs = depth // PAIR
    tile = min(256, width)
    sec, me = lax.axis_index("section"), lax.axis_index("ctx")
    core = lax.rem(me, 2)
    chip = lax.div(me, 2)

    def at(chip_index, core_index):
        return lax.rem(chip_index + 2 * chips, chips) * 2 + core_index

    right, left, sibling = at(chip + 1, core), at(chip - 1, core), at(chip, 1 - core)
    next_sec, prev_sec = lax.rem(sec + 1, sections), lax.rem(sec + sections - 1, sections)
    next_ctx, prev_ctx = lax.rem(me + 1, parts), lax.rem(me + parts - 1, parts)

    barrier = pltpu.get_barrier_semaphore()
    for peer in (left, right, sibling):
        pl.semaphore_signal(barrier, inc=1, device_id=(sec, peer), device_id_type=MESH)
    pl.semaphore_signal(barrier, inc=1, device_id=(prev_sec, me), device_id_type=MESH)
    pl.semaphore_signal(barrier, inc=1, device_id=(prev_sec, prev_ctx), device_id_type=MESH)
    pl.semaphore_wait(barrier, 5)

    relay = pltpu.make_async_remote_copy(
        act.at[0], rows_in, relay_send.at[0], relay_recv.at[0],
        device_id=(next_sec, me), device_id_type=MESH,
    )
    relay_halo = pltpu.make_async_remote_copy(
        act.at[0, pl.ds(tokens - HALO, HALO)], halo_in, relay_send.at[1], relay_recv.at[1],
        device_id=(next_sec, next_ctx), device_id_type=MESH,
    )

    hops = [(chips // 2, chips - 1 - chips // 2), (chips - 1 - chips // 2, chips // 2)]
    sources = [
        in_w.at[0, :, pl.ds(width, width)], in_w.at[0, :, pl.ds(2 * width, width)],
        in_w.at[0, :, pl.ds(0, width)], out_w.at[0],
    ]

    streams = [(0, 0, width), (1, 0, width), (2, 0, width), (3, 0, width)]
    key_value, late = (0, 1), (2, 3)

    def rows_of(owner):
        return pl.ds(pl.multiple_of(owner * depth, depth), depth)

    def ring_copy(stream, source, owner, target):
        kind, first, count = streams[stream]
        return pltpu.make_async_remote_copy(
            source, w.at[kind, rows_of(owner), pl.ds(first, count)],
            ring_send.at[stream], ring_recv.at[stream, owner],
            device_id=(sec, target), device_id_type=MESH,
        )

    def sibling_copy(kind, source, owner):
        return pltpu.make_async_remote_copy(
            source, w.at[kind, rows_of(owner)], pair_send.at[kind], pair_recv.at[kind],
            device_id=(sec, sibling), device_id_type=MESH,
        )

    def ring_start(group):
        for stream in group:
            kind, first, count = streams[stream]
            own = sources[kind].at[:, pl.ds(first, count)]
            for count, target in zip(hops[stream % 2], (right, left)):
                if count:
                    ring_copy(stream, own, me, target).start()
        for kind in sorted({streams[stream][0] for stream in group}):
            sibling_copy(kind, sources[kind], me).start()
            pltpu.make_async_copy(sources[kind], w.at[kind, rows_of(me)], own_sem.at[kind]).start()

    def ring_step(group, step):
        for stream in group:
            kind, first, count = streams[stream]
            ways = ((at(chip - step, core), right), (at(chip + step, core), left))
            for far, (owner, target) in zip(hops[stream % 2], ways):
                if step > far:
                    continue
                here = w.at[kind, rows_of(owner), pl.ds(first, count)]
                pltpu.make_async_copy(here, here, ring_recv.at[stream, owner]).wait()
                if step < far:
                    ring_copy(stream, here, owner, target).start()
                if first + count == width:
                    sibling_copy(kind, w.at[kind, rows_of(owner)], owner).start()

    def ring_finish(kind):
        pltpu.make_async_copy(sources[kind], w.at[kind, rows_of(me)], own_sem.at[kind]).wait()

        landed = w.at[kind, pl.ds(0, chips * depth)]
        pltpu.make_async_copy(landed, landed, pair_recv.at[kind]).wait()

    ring_start(key_value)
    relay.start()
    relay_halo.start()
    ring_start(late)

    loads = [
        pltpu.make_async_copy(source, target, load_sem.at[slot])
        for slot, (source, target) in enumerate(
            [
                (filt.at[0], fil), (g_in, g_all), (d_in, d_all), (tw_cos_in, tw_cos), (tw_sin_in, tw_sin),
                (di_in, di_all), (gi_in, gi_all), (gain_in, gain), (taps_in, taps),
            ]
        )
    ]
    for load in loads:
        load.start()

    def outer_rows(pair, columns_high, columns_low):
        lanes = pl.ds(2 * block * pair, 2 * block)
        for index in range(2):
            rows = pl.ds(index * rows_k, rows_k)
            value = dot(g_hi[rows, :], columns_high) + dot(g_lo[rows, :], columns_high)
            if columns_low is not None:
                value = value + dot(g_hi[rows, :], columns_low)
            outer[rows, lanes] = value

    def inner_rows(group):
        lanes = pl.ds(group * block, block)
        real, imag = outer[pl.ds(0, rows_k), lanes], outer[pl.ds(rows_k, rows_k), lanes]
        cos, sin = tw_cos[...], tw_sin[...]
        turned = jnp.concatenate([real * cos + imag * sin, imag * cos - real * sin], axis=1)
        high, low = split(turned)
        return dot3(high, low, d_hi[...], d_lo[...])

    def filter_outer(pair):
        columns = [
            jnp.concatenate(
                [fil[pl.ds(group * FEW, FEW), pl.ds(n * block, block)] for n in range(parts)], axis=0
            )
            for group in (2 * pair, 2 * pair + 1)
        ]
        high, low = split(jnp.concatenate(columns, axis=1))
        outer_rows(pair, high, low)

    def filter_inner(group):
        spec[group] = inner_rows(group) * (1.0 / (parts * block))

    def norm(values, gain_row):
        values = values.astype(F32)
        scale = lax.rsqrt(jnp.mean(values * values, axis=-1, keepdims=True) + 1e-06)
        return values * scale * gain_row

    def norm_rows():
        wait_loads(7, 2)
        relay.wait_recv()
        relay_halo.wait_recv()
        before = norm(halo_in[...], gain[...])
        normed[pl.ds(0, HALO), :] = jnp.where(me > 0, before, jnp.zeros_like(before)).astype(BF16)
        normed[pl.ds(HALO, tokens), :] = norm(rows_in[...], gain[...]).astype(BF16)

    def wait_loads(first, count):
        for load in loads[first : first + count]:
            load.wait()

    steps = chips // 2
    def split_table(whole, high, low):
        high[...], low[...] = split(whole[...])

    between = [
        lambda: (wait_loads(0, 2), split_table(g_all, g_hi, g_lo)),
        lambda: [filter_outer(pair) for pair in range(pairs)],
        lambda: (wait_loads(2, 3), split_table(d_all, d_hi, d_lo), filter_inner(0), filter_inner(1)),
        lambda: [filter_inner(group) for group in range(2, 2 * pairs)],
        norm_rows,
        lambda: (wait_loads(5, 2), split_table(di_all, di_hi, di_lo), split_table(gi_all, gi_hi, gi_lo)),
    ]
    late_done = 0
    for step in range(1, steps + 1):
        ring_step(key_value, step)
        if between:
            between.pop(0)()
        if 2 <= step < steps:
            late_done += 1
            ring_step(late, late_done)
    for piece in between:
        piece()
    def mixed(kind, column, place):
        columns = pl.ds(pl.multiple_of(column, tile), tile)
        feat[place] = dot(normed[...], w[kind, :, columns])
        base = (0 if kind == 2 else width * (kind + 1)) + column
        weights = [taps[i, :, pl.ds(pl.multiple_of(base, tile), tile)] for i in range(3)]
        value = weights[0] * feat[place, pl.ds(HALO, tokens), :]
        value = value + weights[1] * feat[place, pl.ds(HALO - 1, tokens), :]
        return value + weights[2] * feat[place, pl.ds(HALO - 2, tokens), :]

    tiles = width // tile
    per_tile = tile // depth

    turns = [2, 1, 3, 0] if tiles == 4 else [*range(1, tiles), 0]

    def quarter(turn):
        return lax.rem(lax.div(me, per_tile) + turn, tiles)

    def product_tile(index, carry):
        at_tile = lax.rem(lax.div(me, per_tile) + 2 + index, tiles)
        column = at_tile * tile
        value = (mixed(0, column, 0) * mixed(1, column, 1)).T.astype(BF16)
        first = pl.multiple_of(at_tile * per_tile, per_tile)
        prod[pl.ds(first, per_tile)] = value.reshape(per_tile, depth, tokens)

        lax.fori_loop(0, per_tile, lambda offset, inner: send(0, first + offset, inner), 0, unroll=True)
        return carry

    def over(source, target, send_sem, recv_sem):
        def send(pair, peer, carry):
            channels = pl.ds(pair * PAIR, PAIR)

            @pl.when(peer != me)
            def _():
                pltpu.make_async_remote_copy(
                    source.at[peer, channels], target.at[me, channels], send_sem.at[pair], recv_sem.at[pair],
                    device_id=(sec, peer), device_id_type=MESH,
                ).start()

            return carry

        def here(pair):
            landed = target.at[pl.ds(0, parts - 1), pl.ds(0, PAIR)]
            pltpu.make_async_copy(landed, landed, recv_sem.at[pair]).wait()

        def left_here():
            for pair in range(pairs):
                others = source.at[pl.ds(0, parts - 1), pl.ds(0, PAIR)]
                pltpu.make_async_copy(others, others, send_sem.at[pair]).wait()

        return send, here, left_here

    send, product_here, product_left = over(prod, chan, to_send, to_recv)
    send_back, conv_here, conv_left = over(conv, ret, back_send, back_recv)

    def to_all(send_one, pair):
        for turn in turns:
            first = quarter(turn) * per_tile
            lax.fori_loop(
                0, per_tile,
                lambda offset, carry, first=first: send_one(pair, first + lax.rem(me + offset, per_tile), carry), 0,
                unroll=True,
            )

    ring_finish(0)
    ring_finish(1)
    lax.fori_loop(0, tiles, product_tile, 0)
    chan[me] = prod[me]

    def late_step():
        nonlocal late_done
        if late_done < steps:
            late_done += 1
            ring_step(late, late_done)

    late_step()
    for pair in range(1, pairs):
        to_all(send, pair)


    def convolve(pair):
        data = chan[:, pl.ds(pair * PAIR, PAIR), :].astype(F32)
        columns = jnp.concatenate(
            [data[:, :FEW].reshape(rows_k, block), data[:, FEW:].reshape(rows_k, block)], axis=1
        )
        outer_rows(pair, columns.astype(BF16), None)
        for group in (2 * pair, 2 * pair + 1):
            lanes = pl.ds(group * block, block)
            data = inner_rows(group)
            real, imag = data[:, :block], data[:, block:]
            filter_real, filter_imag = spec[group, :, pl.ds(0, block)], spec[group, :, pl.ds(block, block)]
            points = jnp.concatenate(
                [real * filter_real - imag * filter_imag, real * filter_imag + imag * filter_real], axis=1
            )
            high, low = split(points)
            value = dot3(high, low, di_hi[...], di_lo[...])
            real, imag = value[:, :block], value[:, block:]
            cos, sin = tw_cos[...], tw_sin[...]
            above, below = pl.ds(0, rows_k), pl.ds(rows_k, rows_k)
            back_hi[above, lanes], back_lo[above, lanes] = split(real * cos - imag * sin)
            back_hi[below, lanes], back_lo[below, lanes] = split(imag * cos + real * sin)
        lanes = pl.ds(2 * block * pair, 2 * block)
        value = dot3(gi_hi[...], gi_lo[...], back_hi[:, lanes], back_lo[:, lanes])
        whole = jnp.concatenate(
            [value[:, :block].reshape(parts, FEW, block), value[:, block:].reshape(parts, FEW, block)], axis=1
        )
        conv[:, pl.ds(pair * PAIR, PAIR), :] = whole.astype(BF16)

    for pair in range(pairs):
        product_here(pair)
        convolve(pair)
        to_all(send_back, pair)
        late_step()
    ret[me] = conv[me]
    while late_done < steps:
        late_step()

    def query_tile(index, carry):
        value = mixed(2, index * tile, 0).T
        query[pl.ds(pl.multiple_of(index * per_tile, per_tile), per_tile)] = value.reshape(per_tile, depth, tokens)
        return carry

    ring_finish(2)
    lax.fori_loop(0, tiles, query_tile, 0)
    ring_finish(3)

    for pair in range(pairs):
        conv_here(pair)
    gates = (query[...] * ret[...].astype(F32)).astype(BF16).reshape(width, tokens)
    for index in range(tiles):
        span = pl.ds(index * tile, tile)
        mixing = dot(w[3, span, :], gates)
        out[0, :, span] = (rows_in[:, span].astype(F32) + mixing.T).astype(BF16)

    relay.wait_send()
    relay_halo.wait_send()
    for stream in key_value + late:
        kind, first, count = streams[stream]
        all_sent = w.at[kind, pl.ds(0, (chips - 1) * depth), pl.ds(first, count)]
        pltpu.make_async_copy(all_sent, all_sent, ring_send.at[stream]).wait()
    for kind in range(4):
        all_sent = w.at[kind, pl.ds(0, chips * depth)]
        pltpu.make_async_copy(all_sent, all_sent, pair_send.at[kind]).wait()
    product_left()
    conv_left()


def shards(activations, norm_gain, in_weight, short_weight, long_filter, out_weight):
    sections, parts = lax.axis_size("section"), lax.axis_size("ctx")
    chips = parts // 2
    tokens, width = activations.shape[1:]
    depth = width // parts
    rows_k = parts * FEW
    groups, pairs = depth // FEW, depth // PAIR
    tables = [jnp.asarray(table) for table in transform_tables(parts, tokens)]
    in_hbm = pl.BlockSpec(memory_space=pltpu.HBM)
    in_vmem = pl.BlockSpec(memory_space=pltpu.VMEM)
    tile = min(256, width)
    scratch = [
        pltpu.VMEM((4, width, width), BF16),
        pltpu.VMEM((tokens, width), BF16),
        pltpu.VMEM((HALO, width), BF16),
        pltpu.VMEM((HALO + tokens, width), BF16),
        pltpu.VMEM((2, HALO + tokens, tile), F32),
        pltpu.VMEM((parts, depth, tokens), BF16),
        pltpu.VMEM((parts, depth, tokens), BF16),
        pltpu.VMEM((parts, depth, tokens), F32),
        pltpu.VMEM((2 * rows_k, groups * tokens), F32),
        pltpu.VMEM((groups, rows_k, 2 * tokens), F32),
        pltpu.VMEM((2 * rows_k, groups * tokens), BF16),
        pltpu.VMEM((2 * rows_k, groups * tokens), BF16),
        pltpu.VMEM((parts, depth, tokens), BF16),
        pltpu.VMEM((parts, depth, tokens), BF16),
        pltpu.VMEM(norm_gain.shape, F32),
        pltpu.VMEM((3, 1, 3 * width), F32),
        pltpu.VMEM(long_filter.shape[1:], F32),
        *[pltpu.VMEM(table.shape, F32) for table in tables],
        *[pltpu.VMEM(table.shape, BF16) for table in tables[:4] for _ in range(2)],
        pltpu.SemaphoreType.DMA((4,)),
        pltpu.SemaphoreType.DMA((4, parts)),
        pltpu.SemaphoreType.DMA((4,)),
        pltpu.SemaphoreType.DMA((4,)),
        pltpu.SemaphoreType.DMA((4,)),
        pltpu.SemaphoreType.DMA((2,)),
        pltpu.SemaphoreType.DMA((2,)),
        pltpu.SemaphoreType.DMA((pairs,)),
        pltpu.SemaphoreType.DMA((pairs,)),
        pltpu.SemaphoreType.DMA((pairs,)),
        pltpu.SemaphoreType.DMA((pairs,)),
        pltpu.SemaphoreType.DMA((len(tables) + 3,)),
    ]
    return pl.pallas_call(
        functools.partial(kernel, sections, chips, width, tokens),
        out_shape=pltpu.VMEM(activations.shape, BF16),
        in_specs=[in_hbm] * (6 + len(tables)),
        out_specs=in_vmem,
        scratch_shapes=scratch,
        compiler_params=pltpu.CompilerParams(
            collective_id=0, has_side_effects=True, vmem_limit_bytes=63 * 1024 * 1024
        ),
    )(
        activations, norm_gain, in_weight, jnp.transpose(short_weight, (1, 0, 2)), long_filter,
        jnp.swapaxes(out_weight, 1, 2), *tables,
    )


def solution(mesh):
    return jax.shard_map(
        shards,
        mesh=mesh,
        in_specs=(
            P("section", "ctx", None),
            P("section", None),
            P("section", "ctx", None),
            P("section", None, None),
            P("section", "ctx", None),
            P("section", None, "ctx"),
        ),
        out_specs=P("section", "ctx", None),
        check_vma=False,
    )
```
